32 devices in a mesh: ctx: 8 (over z, x), head: 4 (over y, core).
Axes of the slice: x: 2, y: 2, z: 4, core: 2. Of those that a mesh axis runs over, the one named last changes fastest.
Arguments:
- lin_query: bfloat16 [1024, 8192], P('ctx', 'head'), may hold values from -6 to 6
- lin_key: bfloat16 [1024, 8192], P('ctx', 'head'), may hold values from -6 to 6
- lin_value: bfloat16 [1024, 8192], P('ctx', 'head'), may hold values from -6 to 6
- log_decay: float32 [1024, 64], P('ctx', 'head'), may hold values from -1 to 0, as said below
- soft_query: bfloat16 [1024, 8192], P('ctx', 'head'), may hold values from -24 to 24
- soft_key: bfloat16 [1024, 8192], P('ctx', 'head'), may hold values from -24 to 24
- soft_value: bfloat16 [1024, 8192], P('ctx', 'head'), may hold values from -6 to 6
Outputs:
- lin_out: bfloat16 [1024, 8192], P('ctx', 'head')
- soft_out: bfloat16 [1024, 8192], P('ctx', 'head')
The draws below stay inside these ranges and needn't reach their ends.
Inputs may be any that keep to these rules, and one draw needn't show every extreme that they name: `log_decay`: never positive.
All inputs are finite; a program needn't handle non-finite values.
Results may differ from the reference program's by a relative error of at most 0.0065.
Values may be sent and summed in bfloat16 or wider, within the bound.
A program may use at most 192 MiB of HBM per device.

```python
import jax
import jax.numpy as jnp
from jax import lax

HEADS = 64
HEAD_DIM = 128
TOK_DEV = 128
SEQ = 1024


def soft_pair(key):
    base_key = jax.random.fold_in(key, 11)
    key_query, key_keys = jax.random.split(base_key, 2)
    width_all = HEADS * HEAD_DIM
    queries = jnp.clip(jax.random.normal(key_query, (SEQ, width_all), jnp.float32), -4.0, 4.0)
    keys_all = jnp.clip(jax.random.normal(key_keys, (SEQ, width_all), jnp.float32), -4.0, 4.0)
    return (queries, keys_all)


def draw_soft_query(key, part):
    return soft_pair(key)[0].astype(jnp.bfloat16)


def draw_soft_key(key, part):
    return soft_pair(key)[1].astype(jnp.bfloat16)


def draw_log_decay(key, part):
    base_key = jax.random.fold_in(key, 23)
    key_kind, key_fast, key_slow, key_block, key_token, key_where, key_loss = jax.random.split(base_key, 7)
    fast_share = 0.5
    fast_heads = jax.random.uniform(key_kind, (HEADS,), jnp.float32) < fast_share
    fast_rate = jnp.exp(jax.random.uniform(key_fast, (HEADS,), jnp.float32, jnp.log(0.5), jnp.log(3.0))) / TOK_DEV
    slow_rate = jnp.exp(jax.random.uniform(key_slow, (HEADS,), jnp.float32, jnp.log(0.05), jnp.log(0.3))) / SEQ
    head_rate = jnp.where(fast_heads, fast_rate, slow_rate)
    block_width = jnp.where(fast_heads, jnp.log(4.0), jnp.log(2.0))
    block_unit = jax.random.uniform(key_block, (SEQ // TOK_DEV, HEADS), jnp.float32, -1.0, 1.0)
    block_factor = jnp.exp(block_unit * block_width[None, :])
    block_factor = jnp.repeat(block_factor, TOK_DEV, axis=0)
    token_factor = jnp.exp(jax.random.uniform(key_token, (SEQ, HEADS), jnp.float32, -jnp.log(2.0), jnp.log(2.0)))
    log_retention = jnp.maximum(-head_rate[None, :] * block_factor * token_factor, -0.45)
    third_len = SEQ // 3
    token_slots = jnp.arange(3, dtype=jnp.int32)[:, None] * third_len + jax.random.randint(key_where, (3, HEADS), 0, third_len)
    decay_losses = jax.random.uniform(key_loss, (3, HEADS), jnp.float32, 0.2, 0.4)
    token_positions = jnp.arange(SEQ)[:, None]
    for segment_index in range(3):
        log_retention = log_retention + jnp.where(token_positions == token_slots[segment_index][None, :], jnp.log(1.0 - decay_losses[segment_index])[None, :], 0.0)
    return log_retention


def level_of(stream_key, extent, shards, low, top_value):
    loudness, own = 1.0, jax.random.fold_in(stream_key, 6)
    for axis_at, parts in shards:
        heights = jnp.exp(jax.random.uniform(jax.random.fold_in(own, axis_at), (parts,), jnp.float32, low / len(shards), top_value / len(shards)))
        loudness = loudness * jnp.repeat(heights, extent[axis_at] // parts).reshape([-1 if axis == axis_at else 1 for axis in range(len(extent))])
    return loudness


def normal_values(own_key, shape, scale, most, cuts=(), kind=jnp.bfloat16):
    values = jax.random.normal(own_key, shape, jnp.float32) * scale
    if len(cuts) > 0:
        values = level_of(own_key, shape, cuts, -0.22, 0.18) * values
    return jnp.clip(values, min=-most, max=most).astype(kind)


def setup_inputs(seed: int = 0) -> dict:
    arg_keys = jax.random.split(jax.random.key(seed), 8)
    return {
        "lin_query": normal_values(arg_keys[0], (SEQ, HEADS * HEAD_DIM), 1.0, 6.0, ((0, 8), (1, 4))),
        "lin_key": normal_values(arg_keys[1], (SEQ, HEADS * HEAD_DIM), 1.0, 6.0, ((0, 8), (1, 4))),
        "lin_value": normal_values(arg_keys[2], (SEQ, HEADS * HEAD_DIM), 1.0, 6.0, ((0, 8), (1, 4))),
        "log_decay": draw_log_decay(jax.random.fold_in(arg_keys[7], 71), 0),
        "soft_query": draw_soft_query(jax.random.fold_in(arg_keys[7], 71), 0),
        "soft_key": draw_soft_key(jax.random.fold_in(arg_keys[7], 71), 0),
        "soft_value": normal_values(arg_keys[6], (SEQ, HEADS * HEAD_DIM), 1.0, 6.0, ((0, 8), (1, 4))),
    }


norm_eps = 1e-06
masked_score = -1e+30

def rounded(array):
    return lax.optimization_barrier(array.astype(jnp.bfloat16)).astype(jnp.float32)

def lightning_block(carry_state, packed):
    query_group, key_blk, value_blk, decay_blk = packed
    query_wide = query_group.astype(jnp.float32)
    key_wide = key_blk.astype(jnp.float32)
    value_wide = value_blk.astype(jnp.float32)
    count_rows = decay_blk.shape[0]
    running_sum = jnp.cumsum(decay_blk, axis=0)
    ending = running_sum[-1]
    scores = jnp.einsum('thd,shd->hts', query_wide, key_wide, precision=lax.Precision.HIGHEST)
    causal = jnp.arange(count_rows)[:, None] >= jnp.arange(count_rows)[None, :]
    spread = running_sum.T[:, :, None] - running_sum.T[:, None, :]
    decayed = rounded(jnp.where(causal[None], jnp.exp(jnp.where(causal[None], spread, 0.0)), 0.0) * scores)
    inside = jnp.einsum('hts,shd->thd', decayed, value_wide, precision=lax.Precision.HIGHEST)
    query_scaled = rounded(query_wide * jnp.exp(running_sum)[:, :, None])
    outside = jnp.einsum('thd,hde->the', query_scaled, rounded(carry_state), precision=lax.Precision.HIGHEST)
    to_end = jnp.exp(ending[None, :] - running_sum)
    key_scaled = rounded(key_wide * to_end[:, :, None])
    block_state = jnp.einsum('shd,she->hde', key_scaled, value_wide, precision=lax.Precision.HIGHEST)
    new_state = jnp.exp(ending)[:, None, None] * carry_state + block_state
    total = inside + outside
    normed = total * lax.rsqrt(lax.optimization_barrier(jnp.mean(total * total, axis=-1, keepdims=True)) + norm_eps)
    return (new_state, normed.astype(jnp.bfloat16))

def softmax_head(packed):
    query_one, key_one, value_one = packed
    scores = jnp.dot(query_one, key_one.T, preferred_element_type=jnp.float32) * HEAD_DIM ** (-0.5)
    causal = jnp.arange(SEQ)[:, None] >= jnp.arange(SEQ)[None, :]
    scores = jnp.where(causal, scores, masked_score)
    peak = lax.optimization_barrier(jnp.max(scores, axis=-1, keepdims=True))
    expo = jnp.where(causal, jnp.exp(scores - peak), 0.0)
    weights = expo.astype(jnp.bfloat16)
    numer = jnp.dot(weights, value_one, preferred_element_type=jnp.float32)
    return (numer / lax.optimization_barrier(jnp.sum(expo, axis=-1, keepdims=True))).astype(jnp.bfloat16)

def reference(lin_query, lin_key, lin_value, log_decay, soft_query, soft_key, soft_value):
    blocks_count = SEQ // TOK_DEV
    shaped = (blocks_count, TOK_DEV, HEADS, HEAD_DIM)
    packed = (lin_query.reshape(shaped), lin_key.reshape(shaped), lin_value.reshape(shaped), log_decay.reshape(blocks_count, TOK_DEV, HEADS))
    start_state = jnp.zeros((HEADS, HEAD_DIM, HEAD_DIM), jnp.float32)
    final_state, lin_blocks = lax.scan(lightning_block, start_state, packed)
    lin_out = lin_blocks.reshape(SEQ, HEADS * HEAD_DIM)

    def per_head(array):
        return array.reshape(SEQ, HEADS, HEAD_DIM).transpose(1, 0, 2)
    soft_heads = lax.map(softmax_head, (per_head(soft_query), per_head(soft_key), per_head(soft_value)))
    soft_out = soft_heads.transpose(1, 0, 2).reshape(SEQ, HEADS * HEAD_DIM)
    return (lin_out, soft_out)
```

```python
import functools

import jax
import jax.numpy as jnp
from jax import lax
from jax.experimental import pallas as pl
from jax.experimental.pallas import tpu as pltpu
from jax.sharding import PartitionSpec as P

HEAD_DIM = 128
NORM_EPS = 1e-06
MASKED = -1e30
F32 = jnp.float32
BF16 = jnp.bfloat16


def contract(a, b, dims):
    return lax.dot_general(a, b, (dims, ((), ())), preferred_element_type=F32)


def lanes(index):
    return pl.ds(pl.multiple_of(index * HEAD_DIM, HEAD_DIM), HEAD_DIM)


def kernel(
    n,
    lq, lk, lv, ld, sq, sk, sv,
    lin_out, soft_out,
    qs, ks, vs, qx, os, ox, os_in, ox_in, ls, lx, ls_in, lx_in,
    st, st_in, ends, ends_in, pr, pr_in, tot, tot_in, rst, inside,
    own_sem,
    q_snd, q_rcv, k_snd, k_rcv, v_snd, v_rcv,
    qx_snd, qx_rcv, st_snd, st_rcv, en_snd, en_rcv, tot_snd, tot_rcv,
    pr_snd, pr_rcv, os_snd, os_rcv, ls_snd, ls_rcv, ox_snd, ox_rcv, lx_snd, lx_rcv,
):
    tokens = lq.shape[0]
    heads = ld.shape[1]
    half = n // 2
    hp = heads // half
    width = hp * HEAD_DIM
    me = lax.axis_index("ctx")
    side = me // half
    r = lax.rem(me, half)
    lower = side == 0
    upper = side == 1

    def peer(d):
        return lax.rem(r + d, half)

    def source(d):
        return lax.rem(r + half - d, half)

    def cols(index):
        return pl.ds(pl.multiple_of(index * width, width), width)

    def rows(index):
        if isinstance(index, int):
            return pl.ds(index * tokens, tokens)
        return pl.ds(pl.multiple_of(index * tokens, tokens), tokens)

    def remote(src, dst, snd, rcv, target):
        return pltpu.make_async_remote_copy(
            src_ref=src, dst_ref=dst, send_sem=snd, recv_sem=rcv,
            device_id={"ctx": target}, device_id_type=pl.DeviceIdType.MESH,
        )

    def here(index):
        return side * half + index

    def q_copy(d):
        j = peer(d)
        return remote(sq.at[:, cols(j)], qs.at[rows(r), :], q_snd.at[d], q_rcv.at[d], here(j))

    def k_copy(d):
        j = peer(d)
        return remote(sk.at[:, cols(j)], ks.at[rows(r), :], k_snd.at[d], k_rcv.at[d], here(j))

    def v_copy(d):
        j = peer(d)
        return remote(sv.at[:, cols(j)], vs.at[rows(r), :], v_snd.at[d], v_rcv.at[d], here(j))

    def qx_copy(i, d):
        j = peer(d)
        return remote(
            sq.at[:, lanes(j * hp + i)], qx.at[rows(r), lanes(i)],
            qx_snd.at[i, d], qx_rcv.at[i, d], j,
        )

    def st_copy(d):
        j = peer(d)
        return remote(
            st.at[pl.ds(j * hp, hp)], st_in.at[r], st_snd.at[d], st_rcv.at[d], here(j)
        )

    def en_copy(d):
        return remote(ends, ends_in.at[r], en_snd.at[d], en_rcv.at[d], here(peer(d)))

    def tot_copy():
        return remote(tot, tot_in, tot_snd, tot_rcv, half + r)

    def pr_copy(d):
        j = peer(d)
        return remote(pr.at[j], pr_in.at[r], pr_snd.at[d], pr_rcv.at[d], here(j))

    def os_copy(d):
        j = peer(d)
        return remote(
            os.at[rows(j), :], os_in.at[:, cols(r)], os_snd.at[d], os_rcv.at[d], here(j)
        )

    def ls_copy(d):
        j = peer(d)
        return remote(ls.at[j], ls_in.at[r], ls_snd.at[d], ls_rcv.at[d], here(j))

    def ox_copy(i, j):
        return remote(
            ox.at[rows(j), lanes(i)], ox_in.at[:, lanes(r * hp + i)],
            ox_snd.at[i, j], ox_rcv.at[i, r], half + j,
        )

    def ox_arrival(i, j):
        return remote(
            ox.at[rows(j), lanes(i)], ox_in.at[:, lanes(j * hp + i)],
            ox_snd.at[i, j], ox_rcv.at[i, j], r,
        )

    def lx_copy(j):
        return remote(lx.at[j], lx_in.at[r], lx_snd.at[j], lx_rcv.at[r], half + j)

    def lx_arrival(j):
        return remote(lx.at[j], lx_in.at[j], lx_snd.at[j], lx_rcv.at[j], r)

    others = range(1, half)

    barrier = pltpu.get_barrier_semaphore()
    for step in range(1, n):
        pl.semaphore_signal(
            barrier, inc=1, device_id={"ctx": lax.rem(me + step, n)},
            device_id_type=pl.DeviceIdType.MESH,
        )
    own = [
        pltpu.make_async_copy(sq.at[:, cols(r)], qs.at[rows(r), :], own_sem.at[0]),
        pltpu.make_async_copy(sk.at[:, cols(r)], ks.at[rows(r), :], own_sem.at[1]),
        pltpu.make_async_copy(sv.at[:, cols(r)], vs.at[rows(r), :], own_sem.at[2]),
    ]
    for copy in own:
        copy.start()
    pl.semaphore_wait(barrier, n - 1)

    @pl.when(upper)
    def _():
        for i in range(hp):
            for d in range(half):
                qx_copy(i, d).start()

    for make in (k_copy, v_copy, q_copy):
        for d in others:
            make(d).start()

    at_row = lax.broadcasted_iota(jnp.int32, (tokens, tokens), 0)
    at_col = lax.broadcasted_iota(jnp.int32, (tokens, tokens), 1)
    causal = at_row >= at_col
    padded = jnp.concatenate(
        [ld[...], jnp.zeros((tokens, HEAD_DIM - heads), F32)], axis=1
    )
    running = jnp.dot(
        causal.astype(F32), padded, precision=lax.Precision.HIGHEST, preferred_element_type=F32
    )
    rst[...] = running.T
    ends[...] = jnp.broadcast_to(rst[pl.ds(0, heads), tokens - 1 :], ends.shape)

    def states(h, carry):
        down = jnp.broadcast_to(rst[pl.ds(h, 1), :], (tokens, tokens)).T
        to_end = jnp.exp(down[tokens - 1 :, :] - down)
        scaled = (lk[:, lanes(h)].astype(F32) * to_end).astype(BF16)
        st[h] = contract(scaled, lv[:, lanes(h)], ((0,), (0,))).astype(BF16)
        return carry

    lax.fori_loop(0, heads, states, 0)
    for d in others:
        en_copy(d).start()
        st_copy(d).start()

    def within(h, carry):
        across = jnp.broadcast_to(rst[pl.ds(h, 1), :], (tokens, tokens))
        spread = jnp.where(causal, across.T - across, 0.0)
        scores = contract(lq[:, lanes(h)], lk[:, lanes(h)], ((1,), (1,)))
        decayed = jnp.where(causal, jnp.exp(spread) * scores, 0.0).astype(BF16)
        inside[:, lanes(h)] = contract(decayed, lv[:, lanes(h)], ((1,), (0,)))
        return carry

    lax.fori_loop(0, heads, within, 0)

    def attend(query, keys, values, block):
        scores = contract(query, keys, ((1,), (1,))) * HEAD_DIM ** (-0.5)
        if block is not None:
            row = lax.broadcasted_iota(jnp.int32, scores.shape, 0) + block * tokens
            col = lax.broadcasted_iota(jnp.int32, scores.shape, 1)
            scores = jnp.where(col <= row, scores, MASKED)
        peak = jnp.max(scores, axis=1, keepdims=True)
        expo = jnp.exp(scores - peak)
        mass = jnp.sum(expo, axis=1, keepdims=True)
        result = contract(expo.astype(BF16), values, ((1,), (0,))) / mass
        level = jnp.broadcast_to(peak + jnp.log(mass), (tokens, tokens)).T
        return result.astype(BF16), level[0:1, :]

    def crossing(i, carry):
        for d in range(half):
            qx_copy(i, d).wait_recv()
        keys = ks[:, lanes(i)]
        values = vs[:, lanes(i)]
        for b in range(half):
            result, level = attend(qx[rows(b), lanes(i)], keys, values, None)
            ox[rows(b), lanes(i)] = result
            lx[b, pl.ds(i, 1), :] = level
            ox_copy(i, b).start()
        return carry

    def local(i, carry):
        for b in range(half):
            upto = (b + 1) * tokens
            result, level = attend(
                qs[rows(b), lanes(i)], ks[:upto, lanes(i)], vs[:upto, lanes(i)], b
            )
            os[rows(b), lanes(i)] = result
            ls[b, pl.ds(i, 1), :] = level
        return carry

    def priors():
        for d in others:
            en_copy(d).wait_recv()
            st_copy(d).wait_recv()

        st_in[r] = st[pl.ds(r * hp, hp)]
        ends_in[r] = ends[...]

        def one(i, carry):
            state = jnp.where(upper, tot_in[i].astype(F32), 0.0)
            for c in range(half):
                pr[c, i] = state.astype(BF16)
                keep = jnp.exp(ends_in[c, pl.ds(r * hp + i, 1), :])
                state = keep * state + st_in[c, i].astype(F32)
            tot[i] = state.astype(BF16)
            return carry

        lax.fori_loop(0, hp, one, 0)

    for d in others:
        k_copy(d).wait_recv()
        v_copy(d).wait_recv()
    for copy in own:
        copy.wait()

    @pl.when(lower)
    def _():
        tot_in[...] = jnp.zeros_like(tot_in)
        lax.fori_loop(0, (hp + 1) // 2, crossing, 0)
        priors()
        tot_copy().start()
        lax.fori_loop((hp + 1) // 2, hp, crossing, 0)
        for b in range(half):
            lx_copy(b).start()

    for d in others:
        q_copy(d).wait_recv()
    lax.fori_loop(0, hp, local, 0)
    for d in others:
        os_copy(d).start()
        ls_copy(d).start()

    @pl.when(upper)
    def _():
        tot_copy().wait_recv()
        priors()

    for d in others:
        pr_copy(d).start()
    pr_in[r] = pr[r]
    os_in[:, cols(r)] = os[rows(r), :]
    ls_in[r] = ls[r]

    for d in others:
        pr_copy(d).wait_recv()

    def finish(j, carry):
        def head(i, inner):
            h = j * hp + i
            down = jnp.broadcast_to(rst[pl.ds(h, 1), :], (tokens, tokens)).T
            scaled = (lq[:, lanes(h)].astype(F32) * jnp.exp(down)).astype(BF16)
            total = inside[:, lanes(h)] + contract(scaled, pr_in[j, i], ((1,), (0,)))
            norm = lax.rsqrt(jnp.mean(total * total, axis=1, keepdims=True) + NORM_EPS)
            lin_out[:, lanes(h)] = (total * norm).astype(BF16)
            return inner

        return lax.fori_loop(0, hp, head, carry)

    lax.fori_loop(0, half, finish, 0)

    for d in others:
        os_copy(d).wait_recv()
        ls_copy(d).wait_recv()

    @pl.when(lower)
    def _():
        soft_out[...] = os_in[...]

    @pl.when(upper)
    def _():
        for j in range(half):
            lx_arrival(j).wait_recv()
            for i in range(hp):
                ox_arrival(i, j).wait_recv()

        def merge(j, carry):
            def head(i, inner):
                h = j * hp + i
                gap = lx_in[j, pl.ds(i, 1), :] - ls_in[j, pl.ds(i, 1), :]
                gap = jnp.broadcast_to(gap, (tokens, tokens)).T
                near = 1.0 / (1.0 + jnp.exp(gap))
                far = 1.0 / (1.0 + jnp.exp(-gap))
                mixed = near * os_in[:, lanes(h)].astype(F32)
                mixed = mixed + far * ox_in[:, lanes(h)].astype(F32)
                soft_out[:, lanes(h)] = mixed.astype(BF16)
                return inner

            return lax.fori_loop(0, hp, head, carry)

        lax.fori_loop(0, half, merge, 0)

    for make in (k_copy, v_copy, q_copy, en_copy, st_copy, pr_copy, os_copy, ls_copy):
        for d in others:
            make(d).wait_send()

    @pl.when(upper)
    def _():
        for i in range(hp):
            for d in range(half):
                qx_copy(i, d).wait_send()

    @pl.when(lower)
    def _():
        tot_copy().wait_send()
        for j in range(half):
            lx_copy(j).wait_send()
            for i in range(hp):
                ox_copy(i, j).wait_send()


norm_eps = 1e-06
masked_score = -1e30
key_span = 512
query_span = 512


def entering(value, axis, join, neutral):
    count, mine = (lax.axis_size(axis), lax.axis_index(axis))
    pieces = jax.tree.map(lambda part: lax.all_gather(part, axis), value)
    subtotal = jax.tree.map(
        lambda part, zero: jnp.full_like(part, 0) + jnp.asarray(zero, part.dtype), value, neutral
    )

    def step(position, subtotal):
        longer = join(subtotal, jax.tree.map(lambda part: part[position], pieces))
        return jax.tree.map(lambda new, old: jnp.where(position < mine, new, old), longer, subtotal)

    return lax.fori_loop(0, count - 1, step, subtotal)


def merge_states(earlier, later):
    decay_early, state_early = earlier
    decay_late, state_late = later
    return (decay_early * decay_late, decay_late[:, None, None] * state_early + state_late)


def lightning_core(lin_query, lin_key, lin_value, log_decay):
    tokens = lin_query.shape[0]
    heads_here = log_decay.shape[1]
    query_heads = lin_query.reshape(tokens, heads_here, HEAD_DIM)
    key_heads = lin_key.reshape(tokens, heads_here, HEAD_DIM)
    value_heads = lin_value.reshape(tokens, heads_here, HEAD_DIM)
    running_sum = jnp.cumsum(log_decay, axis=0)
    ending = running_sum[-1]
    scores = jnp.einsum("thd,shd->hts", query_heads, key_heads, preferred_element_type=jnp.float32)
    causal = jnp.arange(tokens)[:, None] >= jnp.arange(tokens)[None, :]
    spread = running_sum.T[:, :, None] - running_sum.T[:, None, :]
    decayed = (
        jnp.where(causal[None], jnp.exp(jnp.where(causal[None], spread, 0.0)), 0.0) * scores
    ).astype(jnp.bfloat16)
    inside = jnp.einsum("hts,shd->thd", decayed, value_heads, preferred_element_type=jnp.float32)
    to_end = jnp.exp(ending[None, :] - running_sum)
    key_scaled = (key_heads.astype(jnp.float32) * to_end[:, :, None]).astype(jnp.bfloat16)
    block_state = jnp.einsum(
        "shd,she->hde", key_scaled, value_heads, preferred_element_type=jnp.float32
    )
    block_decay = jnp.exp(ending)
    before = entering(
        (block_decay, block_state),
        "ctx",
        merge_states,
        (jnp.ones_like(block_decay), jnp.zeros_like(block_state)),
    )
    prior_state = before[1]
    query_scaled = (query_heads.astype(jnp.float32) * jnp.exp(running_sum)[:, :, None]).astype(
        jnp.bfloat16
    )
    outside = jnp.einsum(
        "thd,hde->the",
        query_scaled,
        prior_state.astype(jnp.bfloat16),
        preferred_element_type=jnp.float32,
    )
    total = inside + outside
    normed = total * lax.rsqrt(jnp.mean(total * total, axis=-1, keepdims=True) + norm_eps)
    return normed.reshape(tokens, heads_here * HEAD_DIM).astype(jnp.bfloat16)


def prepare_queries(query_mine, tokens, quarter, head_slot):
    rows_all = query_mine.shape[0]
    heads_now = query_mine.shape[1] // HEAD_DIM
    tile_rows = query_span if rows_all % query_span == 0 else rows_all
    blocks_count = rows_all // tile_rows
    query_blocks = query_mine.reshape(blocks_count, tile_rows, heads_now, HEAD_DIM)
    index_all = jnp.arange(rows_all, dtype=jnp.int32)
    token_slots = index_all // quarter * tokens + head_slot * quarter + index_all % quarter
    initial = (
        jnp.full((blocks_count, tile_rows, heads_now), masked_score, jnp.float32),
        jnp.zeros((blocks_count, tile_rows, heads_now), jnp.float32),
        jnp.zeros((blocks_count, tile_rows, heads_now, HEAD_DIM), jnp.float32),
    )
    return (query_blocks, token_slots.reshape(blocks_count, tile_rows), initial)


def attend_keys(carry, query_blocks, query_places, keys_flat, values_flat, key_places):
    key_total = keys_flat.shape[0]
    heads_now = query_blocks.shape[2]
    keys_heads = keys_flat.reshape(key_total, heads_now, HEAD_DIM)
    values_heads = values_flat.reshape(key_total, heads_now, HEAD_DIM)
    score_scale = HEAD_DIM ** (-0.5)

    def per_block(packed):
        best_start, mass_start, accum_start, query_tile, query_where = packed
        latest_query = jnp.max(query_where)

        def per_span(span_index, running):
            start_row = span_index * key_span
            key_where = lax.dynamic_slice_in_dim(key_places, start_row, key_span, 0)

            def compute(state_now):
                best_now, mass_now, accum_now = state_now
                key_tile = lax.dynamic_slice_in_dim(keys_heads, start_row, key_span, 0)
                value_tile = lax.dynamic_slice_in_dim(values_heads, start_row, key_span, 0)
                scores = (
                    jnp.einsum(
                        "qhd,khd->qhk", query_tile, key_tile, preferred_element_type=jnp.float32
                    )
                    * score_scale
                )
                allowed = (key_where[None, :] <= query_where[:, None])[:, None, :]
                scores = jnp.where(allowed, scores, masked_score)
                best_next = jnp.maximum(best_now, jnp.max(scores, axis=-1))
                expo = jnp.where(allowed, jnp.exp(scores - best_next[:, :, None]), 0.0)
                shrink = jnp.exp(best_now - best_next)
                mass_next = mass_now * shrink + jnp.sum(expo, axis=-1)
                accum_next = accum_now * shrink[:, :, None] + jnp.einsum(
                    "qhk,khd->qhd",
                    expo.astype(jnp.bfloat16),
                    value_tile,
                    preferred_element_type=jnp.float32,
                )
                return (best_next, mass_next, accum_next)

            def unchanged(state_now):
                return state_now

            return lax.cond(jnp.min(key_where) <= latest_query, compute, unchanged, running)

        return lax.fori_loop(
            0, key_total // key_span, per_span, (best_start, mass_start, accum_start)
        )

    return lax.map(per_block, (carry[0], carry[1], carry[2], query_blocks, query_places))


def softmax_core(soft_query, soft_key, soft_value):
    tokens = soft_query.shape[0]
    quarter = tokens // lax.axis_size("head")
    head_slot = lax.axis_index("head")
    query_moved, key_moved, value_moved = (
        lax.all_to_all(soft_query, "head", split_axis=0, concat_axis=1, tiled=True),
        lax.all_to_all(soft_key, "head", split_axis=0, concat_axis=1, tiled=True),
        lax.all_to_all(soft_value, "head", split_axis=0, concat_axis=1, tiled=True),
    )
    query_mine, key_mine, value_mine = (
        lax.all_to_all(query_moved, "ctx", split_axis=1, concat_axis=0, tiled=True),
        lax.all_to_all(key_moved, "ctx", split_axis=1, concat_axis=0, tiled=True),
        lax.all_to_all(value_moved, "ctx", split_axis=1, concat_axis=0, tiled=True),
    )
    query_blocks, query_places, initial = prepare_queries(query_mine, tokens, quarter, head_slot)
    resident_rows = key_mine.shape[0]
    pieces = (
        lax.all_gather(key_mine, "head", axis=0, tiled=True),
        lax.all_gather(value_mine, "head", axis=0, tiled=True),
    )
    key_total = pieces[0].shape[0]
    index_all = jnp.arange(key_total, dtype=jnp.int32)
    source = index_all // resident_rows
    within = index_all % resident_rows
    token_slots = within // quarter * tokens + source * quarter + within % quarter
    result = attend_keys(initial, query_blocks, query_places, pieces[0], pieces[1], token_slots)
    best_final, mass_final, accum_final = result
    outcome = (
        (accum_final / mass_final[..., None]).reshape(query_mine.shape[0], -1).astype(jnp.bfloat16)
    )
    return lax.all_to_all(
        lax.all_to_all(outcome, "ctx", split_axis=0, concat_axis=1, tiled=True),
        "head",
        split_axis=1,
        concat_axis=0,
        tiled=True,
    )


def plain_shards(lin_query, lin_key, lin_value, log_decay, soft_query, soft_key, soft_value):
    lin_out = lightning_core(lin_query, lin_key, lin_value, log_decay)
    soft_out = softmax_core(soft_query, soft_key, soft_value)
    return (lin_out, soft_out)


def shards(lin_query, lin_key, lin_value, log_decay, soft_query, soft_key, soft_value):
    n = lax.axis_size("ctx")
    tokens, columns = lin_query.shape
    heads = log_decay.shape[1]
    half = n // 2
    hp = heads // half
    width = hp * HEAD_DIM
    level_rows = -(-hp // 8) * 8
    vmem = pl.BlockSpec(memory_space=pltpu.VMEM)
    far = pl.BlockSpec(memory_space=pl.ANY)
    big = pltpu.VMEM((half * tokens, width), BF16)
    full = pltpu.VMEM((tokens, columns), BF16)
    level = pltpu.VMEM((half, level_rows, tokens), F32)
    grid_states = pltpu.VMEM((half, hp, HEAD_DIM, HEAD_DIM), BF16)
    some_states = pltpu.VMEM((hp, HEAD_DIM, HEAD_DIM), BF16)
    dma = pltpu.SemaphoreType.DMA
    ring = [dma((half,)), dma((half,))]
    square = [dma((hp, half)), dma((hp, half))]
    single = [dma, dma]
    return pl.pallas_call(
        functools.partial(kernel, n),
        out_shape=[jax.ShapeDtypeStruct((tokens, columns), BF16)] * 2,
        in_specs=[vmem] * 4 + [far] * 3,
        out_specs=[vmem] * 2,
        scratch_shapes=[big] * 6 + [full] * 2 + [level] * 4
        + [
            pltpu.VMEM((heads, HEAD_DIM, HEAD_DIM), BF16),
            grid_states,
            pltpu.VMEM((heads, tokens), F32),
            pltpu.VMEM((half, heads, tokens), F32),
            grid_states,
            grid_states,
            some_states,
            some_states,
            pltpu.VMEM((HEAD_DIM, tokens), F32),
            pltpu.VMEM((tokens, columns), F32),
            dma((3,)),
        ]
        + ring * 3 + square + ring * 2 + single + ring * 3 + square + ring,
        compiler_params=pltpu.CompilerParams(
            collective_id=0, has_side_effects=True, vmem_limit_bytes=40 * 1024 * 1024
        ),
        cost_estimate=pl.CostEstimate(
            flops=3 * 10**9, bytes_accessed=4 * 10**6, transcendentals=3 * 10**6
        ),
    )(lin_query, lin_key, lin_value, log_decay, soft_query, soft_key, soft_value)


def solution(mesh):
    spec = P("ctx", "head")
    n = mesh.shape["ctx"]

    def body(*args):
        heads = args[3].shape[1]
        if n % 2 or n < 4 or heads % (n // 2):
            return plain_shards(*args)
        return shards(*args)

    return jax.shard_map(
        body, mesh=mesh, in_specs=(spec,) * 7, out_specs=(spec,) * 2, check_vma=False
    )
```

```python
import functools

import jax
import jax.numpy as jnp
from jax import lax
from jax.experimental import pallas as pl
from jax.experimental.pallas import tpu as pltpu
from jax.sharding import PartitionSpec as P

HEAD_DIM = 128
NORM_EPS = 1e-06
MASKED = -1e30
SCORE_SCALE = HEAD_DIM ** (-0.5) * 1.4426950408889634
F32 = jnp.float32
BF16 = jnp.bfloat16


def contract(a, b, dims):
    return lax.dot_general(a, b, (dims, ((), ())), preferred_element_type=F32)


def lanes(index):
    return pl.ds(pl.multiple_of(index * HEAD_DIM, HEAD_DIM), HEAD_DIM)


def kernel(
    n,
    lq_far, lk_far, lv_far, ld, sq, sk, sv,
    lin_out, soft_out,
    lq, lk, lv, qs, ks, vs, qx, os, ox, os_in, ox_in, ls, lx, ls_in, lx_in,
    st, st_in, ends, ends_in, pr, pr_in, tot, tot_in, rst, inside,
    own_sem,
    q_snd, q_rcv, k_snd, k_rcv, v_snd, v_rcv,
    qx_snd, qx_rcv, st_snd, st_rcv, en_snd, en_rcv, tot_snd, tot_rcv,
    pr_snd, pr_rcv, os_snd, os_rcv, ls_snd, ls_rcv, ox_snd, ox_rcv, lx_snd, lx_rcv,
):
    tokens = lq.shape[0]
    heads = ld.shape[0]
    half = n // 2
    hp = heads // half
    width = hp * HEAD_DIM
    me = lax.axis_index("ctx")
    side = me // half
    r = lax.rem(me, half)
    lower = side == 0
    upper = side == 1

    def peer(d):
        return lax.rem(r + d, half)

    def source(d):
        return lax.rem(r + half - d, half)

    def cols(index):
        return pl.ds(pl.multiple_of(index * width, width), width)

    def rows(index):
        if isinstance(index, int):
            return pl.ds(index * tokens, tokens)
        return pl.ds(pl.multiple_of(index * tokens, tokens), tokens)

    def remote(src, dst, snd, rcv, target):
        return pltpu.make_async_remote_copy(
            src_ref=src, dst_ref=dst, send_sem=snd, recv_sem=rcv,
            device_id={"ctx": target}, device_id_type=pl.DeviceIdType.MESH,
        )

    def here(index):
        return side * half + index

    def q_copy(d):
        j = peer(d)
        return remote(sq.at[:, cols(j)], qs.at[rows(r), :], q_snd.at[d], q_rcv.at[d], here(j))

    def k_copy(d):
        j = peer(d)
        return remote(sk.at[:, cols(j)], ks.at[rows(r), :], k_snd.at[d], k_rcv.at[d], here(j))

    def v_copy(d):
        j = peer(d)
        return remote(sv.at[:, cols(j)], vs.at[rows(r), :], v_snd.at[d], v_rcv.at[d], here(j))

    def qx_copy(i, d):
        j = peer(d)
        return remote(
            sq.at[:, lanes(j * hp + i)], qx.at[rows(r), lanes(i)],
            qx_snd.at[i, d], qx_rcv.at[i, d], j,
        )

    def st_copy(d):
        j = peer(d)
        return remote(
            st.at[pl.ds(j * hp, hp)], st_in.at[r], st_snd.at[d], st_rcv.at[d], here(j)
        )

    def en_copy(d):
        return remote(ends, ends_in.at[r], en_snd.at[d], en_rcv.at[d], here(peer(d)))

    def tot_copy():
        return remote(tot, tot_in, tot_snd, tot_rcv, half + r)

    def pr_copy(d):
        j = peer(d)
        return remote(pr.at[j], pr_in.at[r], pr_snd.at[d], pr_rcv.at[d], here(j))

    def os_copy(d):
        j = peer(d)
        return remote(
            os.at[rows(j), :], os_in.at[:, cols(r)], os_snd.at[d], os_rcv.at[d], here(j)
        )

    def ls_copy(d):
        j = peer(d)
        return remote(ls.at[j], ls_in.at[r], ls_snd.at[d], ls_rcv.at[d], here(j))

    def ox_copy(i, j):
        return remote(
            ox.at[rows(j), lanes(i)], ox_in.at[:, lanes(r * hp + i)],
            ox_snd.at[i, j], ox_rcv.at[i, r], half + j,
        )

    def ox_arrival(i, j):
        return remote(
            ox.at[rows(j), lanes(i)], ox_in.at[:, lanes(j * hp + i)],
            ox_snd.at[i, j], ox_rcv.at[i, j], r,
        )

    def lx_copy(j):
        return remote(lx.at[j], lx_in.at[r], lx_snd.at[j], lx_rcv.at[r], half + j)

    def lx_arrival(j):
        return remote(lx.at[j], lx_in.at[j], lx_snd.at[j], lx_rcv.at[j], r)

    others = range(1, half)

    barrier = pltpu.get_barrier_semaphore()
    for step in range(1, n):
        pl.semaphore_signal(
            barrier, inc=1, device_id={"ctx": lax.rem(me + step, n)},
            device_id_type=pl.DeviceIdType.MESH,
        )
    own = [
        pltpu.make_async_copy(lk_far, lk, own_sem.at[3]),
        pltpu.make_async_copy(lv_far, lv, own_sem.at[4]),
        pltpu.make_async_copy(lq_far, lq, own_sem.at[5]),
        pltpu.make_async_copy(sq.at[:, cols(r)], qs.at[rows(r), :], own_sem.at[0]),
        pltpu.make_async_copy(sk.at[:, cols(r)], ks.at[rows(r), :], own_sem.at[1]),
        pltpu.make_async_copy(sv.at[:, cols(r)], vs.at[rows(r), :], own_sem.at[2]),
    ]
    for copy in own:
        copy.start()
    pl.semaphore_wait(barrier, n - 1)

    @pl.when(upper)
    def _():
        for i in range(hp):
            for d in range(half):
                qx_copy(i, d).start()

    for make in (k_copy, v_copy, q_copy):
        for d in others:
            make(d).start()

    at_row = lax.broadcasted_iota(jnp.int32, (tokens, tokens), 0)
    at_col = lax.broadcasted_iota(jnp.int32, (tokens, tokens), 1)
    causal = at_row >= at_col
    rst[...] = jnp.dot(
        ld[...], (at_row <= at_col).astype(F32),
        precision=lax.Precision.HIGHEST, preferred_element_type=F32,
    )
    for copy in own[:3]:
        copy.wait()
    ends[...] = jnp.broadcast_to(rst[:, tokens - 1 :], ends.shape)

    def states(h, carry):
        down = jnp.broadcast_to(rst[pl.ds(h, 1), :], (tokens, tokens)).T
        to_end = jnp.exp(down[tokens - 1 :, :] - down)
        scaled = (lk[:, lanes(h)].astype(F32) * to_end).astype(BF16)
        st[h] = contract(scaled, lv[:, lanes(h)], ((0,), (0,))).astype(BF16)
        return carry

    lax.fori_loop(0, heads, states, 0, unroll=4)
    for d in others:
        en_copy(d).start()
        st_copy(d).start()

    def within(h, carry):
        across = jnp.broadcast_to(rst[pl.ds(h, 1), :], (tokens, tokens))
        spread = jnp.where(causal, across.T - across, 0.0)
        scores = contract(lq[:, lanes(h)], lk[:, lanes(h)], ((1,), (1,)))
        decayed = jnp.where(causal, jnp.exp(spread) * scores, 0.0).astype(BF16)
        inside[:, lanes(h)] = contract(decayed, lv[:, lanes(h)], ((1,), (0,)))
        return carry

    lax.fori_loop(0, heads, within, 0, unroll=4)

    def attend(query, keys, values, block):
        scores = contract(query, keys, ((1,), (1,)))
        if block is not None:
            row = lax.broadcasted_iota(jnp.int32, scores.shape, 0) + block * tokens
            col = lax.broadcasted_iota(jnp.int32, scores.shape, 1)
            scores = jnp.where(col <= row, scores, MASKED)
        peak = jnp.max(scores, axis=1, keepdims=True) * SCORE_SCALE
        expo = jnp.exp2(scores * SCORE_SCALE - peak)
        mass = jnp.sum(expo, axis=1, keepdims=True)
        result = contract(expo.astype(BF16), values, ((1,), (0,))) * (1.0 / mass)
        level = jnp.broadcast_to(peak + jnp.log2(mass), (tokens, tokens)).T
        return result.astype(BF16), level[0:1, :]

    def crossing(i, carry):
        for d in range(half):
            qx_copy(i, d).wait_recv()
        keys = ks[:, lanes(i)]
        values = vs[:, lanes(i)]
        for b in range(half):
            result, level = attend(qx[rows(b), lanes(i)], keys, values, None)
            ox[rows(b), lanes(i)] = result
            lx[b, pl.ds(i, 1), :] = level
        for b in range(half):
            ox_copy(i, b).start()
        return carry

    def local(i, carry):
        for b in range(half):
            upto = (b + 1) * tokens
            result, level = attend(
                qs[rows(b), lanes(i)], ks[:upto, lanes(i)], vs[:upto, lanes(i)], b
            )
            os[rows(b), lanes(i)] = result
            ls[b, pl.ds(i, 1), :] = level
        return carry

    def priors():
        for d in others:
            en_copy(d).wait_recv()
            st_copy(d).wait_recv()

        st_in[r] = st[pl.ds(r * hp, hp)]
        ends_in[r] = ends[...]

        def one(i, carry):
            state = jnp.where(upper, tot_in[i].astype(F32), 0.0)
            for c in range(half):
                pr[c, i] = state.astype(BF16)
                keep = jnp.exp(ends_in[c, pl.ds(r * hp + i, 1), :])
                state = keep * state + st_in[c, i].astype(F32)
            tot[i] = state.astype(BF16)
            return carry

        lax.fori_loop(0, hp, one, 0, unroll=2)

    for d in others:
        k_copy(d).wait_recv()
        v_copy(d).wait_recv()
    for copy in own[3:]:
        copy.wait()

    @pl.when(lower)
    def _():
        tot_in[...] = jnp.zeros_like(tot_in)
        lax.fori_loop(0, (hp + 1) // 2, crossing, 0)
        priors()
        tot_copy().start()
        lax.fori_loop((hp + 1) // 2, hp, crossing, 0)
        for b in range(half):
            lx_copy(b).start()

    for d in others:
        q_copy(d).wait_recv()
    lax.fori_loop(0, hp, local, 0)
    for d in others:
        os_copy(d).start()
        ls_copy(d).start()

    @pl.when(upper)
    def _():
        tot_copy().wait_recv()
        priors()

    for d in others:
        pr_copy(d).start()
    pr_in[r] = pr[r]
    os_in[:, cols(r)] = os[rows(r), :]
    ls_in[r] = ls[r]

    for d in others:
        pr_copy(d).wait_recv()

    def finish(j, carry):
        def head(i, inner):
            h = j * hp + i
            down = jnp.broadcast_to(rst[pl.ds(h, 1), :], (tokens, tokens)).T
            scaled = (lq[:, lanes(h)].astype(F32) * jnp.exp(down)).astype(BF16)
            total = inside[:, lanes(h)] + contract(scaled, pr_in[j, i], ((1,), (0,)))
            norm = lax.rsqrt(jnp.mean(total * total, axis=1, keepdims=True) + NORM_EPS)
            lin_out[:, lanes(h)] = (total * norm).astype(BF16)
            return inner

        return lax.fori_loop(0, hp, head, carry, unroll=True)

    lax.fori_loop(0, half, finish, 0)

    for d in others:
        os_copy(d).wait_recv()
        ls_copy(d).wait_recv()

    @pl.when(lower)
    def _():
        soft_out[...] = os_in[...]

    @pl.when(upper)
    def _():
        for j in range(half):
            lx_arrival(j).wait_recv()
            for i in range(hp):
                ox_arrival(i, j).wait_recv()

        def merge(j, carry):
            def head(i, inner):
                h = j * hp + i
                gap = lx_in[j, pl.ds(i, 1), :] - ls_in[j, pl.ds(i, 1), :]
                gap = jnp.broadcast_to(gap, (tokens, tokens)).T
                near = 1.0 / (1.0 + jnp.exp2(gap))
                far = 1.0 / (1.0 + jnp.exp2(-gap))
                mixed = near * os_in[:, lanes(h)].astype(F32)
                mixed = mixed + far * ox_in[:, lanes(h)].astype(F32)
                soft_out[:, lanes(h)] = mixed.astype(BF16)
                return inner

            return lax.fori_loop(0, hp, head, carry, unroll=True)

        lax.fori_loop(0, half, merge, 0)

    for make in (k_copy, v_copy, q_copy, en_copy, st_copy, pr_copy, os_copy, ls_copy):
        for d in others:
            make(d).wait_send()

    @pl.when(upper)
    def _():
        for i in range(hp):
            for d in range(half):
                qx_copy(i, d).wait_send()

    @pl.when(lower)
    def _():
        tot_copy().wait_send()
        for j in range(half):
            lx_copy(j).wait_send()
            for i in range(hp):
                ox_copy(i, j).wait_send()


norm_eps = 1e-06
masked_score = -1e30
key_span = 512
query_span = 512


def entering(value, axis, join, neutral):
    count, mine = (lax.axis_size(axis), lax.axis_index(axis))
    pieces = jax.tree.map(lambda part: lax.all_gather(part, axis), value)
    subtotal = jax.tree.map(
        lambda part, zero: jnp.full_like(part, 0) + jnp.asarray(zero, part.dtype), value, neutral
    )

    def step(position, subtotal):
        longer = join(subtotal, jax.tree.map(lambda part: part[position], pieces))
        return jax.tree.map(lambda new, old: jnp.where(position < mine, new, old), longer, subtotal)

    return lax.fori_loop(0, count - 1, step, subtotal)


def merge_states(earlier, later):
    decay_early, state_early = earlier
    decay_late, state_late = later
    return (decay_early * decay_late, decay_late[:, None, None] * state_early + state_late)


def lightning_core(lin_query, lin_key, lin_value, log_decay):
    tokens = lin_query.shape[0]
    heads_here = log_decay.shape[1]
    query_heads = lin_query.reshape(tokens, heads_here, HEAD_DIM)
    key_heads = lin_key.reshape(tokens, heads_here, HEAD_DIM)
    value_heads = lin_value.reshape(tokens, heads_here, HEAD_DIM)
    running_sum = jnp.cumsum(log_decay, axis=0)
    ending = running_sum[-1]
    scores = jnp.einsum("thd,shd->hts", query_heads, key_heads, preferred_element_type=jnp.float32)
    causal = jnp.arange(tokens)[:, None] >= jnp.arange(tokens)[None, :]
    spread = running_sum.T[:, :, None] - running_sum.T[:, None, :]
    decayed = (
        jnp.where(causal[None], jnp.exp(jnp.where(causal[None], spread, 0.0)), 0.0) * scores
    ).astype(jnp.bfloat16)
    inside = jnp.einsum("hts,shd->thd", decayed, value_heads, preferred_element_type=jnp.float32)
    to_end = jnp.exp(ending[None, :] - running_sum)
    key_scaled = (key_heads.astype(jnp.float32) * to_end[:, :, None]).astype(jnp.bfloat16)
    block_state = jnp.einsum(
        "shd,she->hde", key_scaled, value_heads, preferred_element_type=jnp.float32
    )
    block_decay = jnp.exp(ending)
    before = entering(
        (block_decay, block_state),
        "ctx",
        merge_states,
        (jnp.ones_like(block_decay), jnp.zeros_like(block_state)),
    )
    prior_state = before[1]
    query_scaled = (query_heads.astype(jnp.float32) * jnp.exp(running_sum)[:, :, None]).astype(
        jnp.bfloat16
    )
    outside = jnp.einsum(
        "thd,hde->the",
        query_scaled,
        prior_state.astype(jnp.bfloat16),
        preferred_element_type=jnp.float32,
    )
    total = inside + outside
    normed = total * lax.rsqrt(jnp.mean(total * total, axis=-1, keepdims=True) + norm_eps)
    return normed.reshape(tokens, heads_here * HEAD_DIM).astype(jnp.bfloat16)


def prepare_queries(query_mine, tokens, quarter, head_slot):
    rows_all = query_mine.shape[0]
    heads_now = query_mine.shape[1] // HEAD_DIM
    tile_rows = query_span if rows_all % query_span == 0 else rows_all
    blocks_count = rows_all // tile_rows
    query_blocks = query_mine.reshape(blocks_count, tile_rows, heads_now, HEAD_DIM)
    index_all = jnp.arange(rows_all, dtype=jnp.int32)
    token_slots = index_all // quarter * tokens + head_slot * quarter + index_all % quarter
    initial = (
        jnp.full((blocks_count, tile_rows, heads_now), masked_score, jnp.float32),
        jnp.zeros((blocks_count, tile_rows, heads_now), jnp.float32),
        jnp.zeros((blocks_count, tile_rows, heads_now, HEAD_DIM), jnp.float32),
    )
    return (query_blocks, token_slots.reshape(blocks_count, tile_rows), initial)


def attend_keys(carry, query_blocks, query_places, keys_flat, values_flat, key_places):
    key_total = keys_flat.shape[0]
    heads_now = query_blocks.shape[2]
    keys_heads = keys_flat.reshape(key_total, heads_now, HEAD_DIM)
    values_heads = values_flat.reshape(key_total, heads_now, HEAD_DIM)
    score_scale = HEAD_DIM ** (-0.5)

    def per_block(packed):
        best_start, mass_start, accum_start, query_tile, query_where = packed
        latest_query = jnp.max(query_where)

        def per_span(span_index, running):
            start_row = span_index * key_span
            key_where = lax.dynamic_slice_in_dim(key_places, start_row, key_span, 0)

            def compute(state_now):
                best_now, mass_now, accum_now = state_now
                key_tile = lax.dynamic_slice_in_dim(keys_heads, start_row, key_span, 0)
                value_tile = lax.dynamic_slice_in_dim(values_heads, start_row, key_span, 0)
                scores = (
                    jnp.einsum(
                        "qhd,khd->qhk", query_tile, key_tile, preferred_element_type=jnp.float32
                    )
                    * score_scale
                )
                allowed = (key_where[None, :] <= query_where[:, None])[:, None, :]
                scores = jnp.where(allowed, scores, masked_score)
                best_next = jnp.maximum(best_now, jnp.max(scores, axis=-1))
                expo = jnp.where(allowed, jnp.exp(scores - best_next[:, :, None]), 0.0)
                shrink = jnp.exp(best_now - best_next)
                mass_next = mass_now * shrink + jnp.sum(expo, axis=-1)
                accum_next = accum_now * shrink[:, :, None] + jnp.einsum(
                    "qhk,khd->qhd",
                    expo.astype(jnp.bfloat16),
                    value_tile,
                    preferred_element_type=jnp.float32,
                )
                return (best_next, mass_next, accum_next)

            def unchanged(state_now):
                return state_now

            return lax.cond(jnp.min(key_where) <= latest_query, compute, unchanged, running)

        return lax.fori_loop(
            0, key_total // key_span, per_span, (best_start, mass_start, accum_start)
        )

    return lax.map(per_block, (carry[0], carry[1], carry[2], query_blocks, query_places))


def softmax_core(soft_query, soft_key, soft_value):
    tokens = soft_query.shape[0]
    quarter = tokens // lax.axis_size("head")
    head_slot = lax.axis_index("head")
    query_moved, key_moved, value_moved = (
        lax.all_to_all(soft_query, "head", split_axis=0, concat_axis=1, tiled=True),
        lax.all_to_all(soft_key, "head", split_axis=0, concat_axis=1, tiled=True),
        lax.all_to_all(soft_value, "head", split_axis=0, concat_axis=1, tiled=True),
    )
    query_mine, key_mine, value_mine = (
        lax.all_to_all(query_moved, "ctx", split_axis=1, concat_axis=0, tiled=True),
        lax.all_to_all(key_moved, "ctx", split_axis=1, concat_axis=0, tiled=True),
        lax.all_to_all(value_moved, "ctx", split_axis=1, concat_axis=0, tiled=True),
    )
    query_blocks, query_places, initial = prepare_queries(query_mine, tokens, quarter, head_slot)
    resident_rows = key_mine.shape[0]
    pieces = (
        lax.all_gather(key_mine, "head", axis=0, tiled=True),
        lax.all_gather(value_mine, "head", axis=0, tiled=True),
    )
    key_total = pieces[0].shape[0]
    index_all = jnp.arange(key_total, dtype=jnp.int32)
    source = index_all // resident_rows
    within = index_all % resident_rows
    token_slots = within // quarter * tokens + source * quarter + within % quarter
    result = attend_keys(initial, query_blocks, query_places, pieces[0], pieces[1], token_slots)
    best_final, mass_final, accum_final = result
    outcome = (
        (accum_final / mass_final[..., None]).reshape(query_mine.shape[0], -1).astype(jnp.bfloat16)
    )
    return lax.all_to_all(
        lax.all_to_all(outcome, "ctx", split_axis=0, concat_axis=1, tiled=True),
        "head",
        split_axis=1,
        concat_axis=0,
        tiled=True,
    )


def plain_shards(lin_query, lin_key, lin_value, log_decay, soft_query, soft_key, soft_value):
    lin_out = lightning_core(lin_query, lin_key, lin_value, log_decay)
    soft_out = softmax_core(soft_query, soft_key, soft_value)
    return (lin_out, soft_out)


def shards(lin_query, lin_key, lin_value, log_decay, soft_query, soft_key, soft_value):
    n = lax.axis_size("ctx")
    tokens, columns = lin_query.shape
    heads = log_decay.shape[1]
    half = n // 2
    hp = heads // half
    width = hp * HEAD_DIM
    level_rows = -(-hp // 8) * 8
    vmem = pl.BlockSpec(memory_space=pltpu.VMEM)
    far = pl.BlockSpec(memory_space=pltpu.HBM)
    big = pltpu.VMEM((half * tokens, width), BF16)
    full = pltpu.VMEM((tokens, columns), BF16)
    level = pltpu.VMEM((half, level_rows, tokens), F32)
    grid_states = pltpu.VMEM((half, hp, HEAD_DIM, HEAD_DIM), BF16)
    some_states = pltpu.VMEM((hp, HEAD_DIM, HEAD_DIM), BF16)
    dma = pltpu.SemaphoreType.DMA
    ring = [dma((half,)), dma((half,))]
    square = [dma((hp, half)), dma((hp, half))]
    single = [dma, dma]
    return pl.pallas_call(
        functools.partial(kernel, n),
        out_shape=[jax.ShapeDtypeStruct((tokens, columns), BF16)] * 2,
        in_specs=[far] * 3 + [vmem] + [far] * 3,
        out_specs=[vmem] * 2,
        scratch_shapes=[full] * 3 + [big] * 6 + [full] * 2 + [level] * 4
        + [
            pltpu.VMEM((heads, HEAD_DIM, HEAD_DIM), BF16),
            grid_states,
            pltpu.VMEM((heads, tokens), F32),
            pltpu.VMEM((half, heads, tokens), F32),
            grid_states,
            grid_states,
            some_states,
            some_states,
            pltpu.VMEM((heads, tokens), F32),
            pltpu.VMEM((tokens, columns), F32),
            dma((6,)),
        ]
        + ring * 3 + square + ring * 2 + single + ring * 3 + square + ring,
        compiler_params=pltpu.CompilerParams(
            collective_id=0, has_side_effects=True, vmem_limit_bytes=60 * 1024 * 1024
        ),
        cost_estimate=pl.CostEstimate(
            flops=3 * 10**9, bytes_accessed=4 * 10**6, transcendentals=3 * 10**6
        ),
    )(lin_query, lin_key, lin_value, log_decay.T, soft_query, soft_key, soft_value)


def solution(mesh):
    spec = P("ctx", "head")
    n = mesh.shape["ctx"]

    def body(*args):
        heads = args[3].shape[1]
        if n % 2 or n < 4 or heads % (n // 2):
            return plain_shards(*args)
        return shards(*args)

    return jax.shard_map(
        body, mesh=mesh, in_specs=(spec,) * 7, out_specs=(spec,) * 2, check_vma=False
    )
```

```python
import functools

import jax
import jax.numpy as jnp
from jax import lax
from jax.experimental import pallas as pl
from jax.experimental.pallas import tpu as pltpu
from jax.sharding import PartitionSpec as P

HEAD_DIM = 128
NORM_EPS = 1e-06
MASKED = -1e30
SCORE_SCALE = HEAD_DIM ** (-0.5) * 1.4426950408889634
F32 = jnp.float32
BF16 = jnp.bfloat16


def contract(a, b, dims):
    return lax.dot_general(a, b, (dims, ((), ())), preferred_element_type=F32)


def lanes(index):
    return pl.ds(pl.multiple_of(index * HEAD_DIM, HEAD_DIM), HEAD_DIM)


def kernel(
    n,
    lq_far, lk_far, lv_far, ld, sq, sk, sv,
    lin_out, soft_out,
    lq, lk, lv, qs, ks, vs, qx, os, ox, os_in, ox_in, ls, lx, ls_in, lx_in,
    st, st_in, ends, ends_in, pr, pr_in, tot, tot_in, rst, inside,
    own_sem,
    q_snd, q_rcv, k_snd, k_rcv, v_snd, v_rcv,
    qx_snd, qx_rcv, st_snd, st_rcv, en_snd, en_rcv, tot_snd, tot_rcv,
    pr_snd, pr_rcv, os_snd, os_rcv, ls_snd, ls_rcv, ox_snd, ox_rcv, lx_snd, lx_rcv,
):
    tokens = lq.shape[0]
    heads = ld.shape[0]
    half = n // 2
    hp = heads // half
    width = hp * HEAD_DIM
    me = lax.axis_index("ctx")
    side = me // half
    r = lax.rem(me, half)
    lower = side == 0
    upper = side == 1

    def peer(d):
        return lax.rem(r + d, half)

    def source(d):
        return lax.rem(r + half - d, half)

    def cols(index):
        return pl.ds(pl.multiple_of(index * width, width), width)

    def rows(index):
        if isinstance(index, int):
            return pl.ds(index * tokens, tokens)
        return pl.ds(pl.multiple_of(index * tokens, tokens), tokens)

    def remote(src, dst, snd, rcv, target):
        return pltpu.make_async_remote_copy(
            src_ref=src, dst_ref=dst, send_sem=snd, recv_sem=rcv,
            device_id={"ctx": target}, device_id_type=pl.DeviceIdType.MESH,
        )

    def here(index):
        return side * half + index

    def q_copy(i, d):
        j = peer(d)
        return remote(
            sq.at[:, lanes(j * hp + i)], qs.at[rows(r), lanes(i)],
            q_snd.at[i, d], q_rcv.at[i, d], here(j),
        )

    def k_copy(i, d):
        j = peer(d)
        return remote(
            sk.at[:, lanes(j * hp + i)], ks.at[rows(r), lanes(i)],
            k_snd.at[i, d], k_rcv.at[i, d], here(j),
        )

    def v_copy(i, d):
        j = peer(d)
        return remote(
            sv.at[:, lanes(j * hp + i)], vs.at[rows(r), lanes(i)],
            v_snd.at[i, d], v_rcv.at[i, d], here(j),
        )

    def qx_copy(i, d):
        j = peer(d)
        return remote(
            sq.at[:, lanes(j * hp + i)], qx.at[rows(r), lanes(i)],
            qx_snd.at[i, d], qx_rcv.at[i, d], j,
        )

    def st_copy(d):
        j = peer(d)
        return remote(
            st.at[pl.ds(j * hp, hp)], st_in.at[r], st_snd.at[d], st_rcv.at[d], here(j)
        )

    def en_copy(d):
        return remote(ends, ends_in.at[r], en_snd.at[d], en_rcv.at[d], here(peer(d)))

    def tot_copy():
        return remote(tot, tot_in, tot_snd, tot_rcv, half + r)

    def pr_copy(d):
        j = peer(d)
        return remote(pr.at[j], pr_in.at[r], pr_snd.at[d], pr_rcv.at[d], here(j))

    def os_copy(i, d):
        j = peer(d)
        return remote(
            os.at[rows(j), lanes(i)], os_in.at[:, lanes(r * hp + i)],
            os_snd.at[i, d], os_rcv.at[i, d], here(j),
        )

    def os_arrival(i, d):
        j = source(d)
        return remote(
            os.at[rows(j), lanes(i)], os_in.at[:, lanes(j * hp + i)],
            os_snd.at[i, d], os_rcv.at[i, d], here(j),
        )

    def ls_copy(d):
        j = peer(d)
        return remote(ls.at[j], ls_in.at[r], ls_snd.at[d], ls_rcv.at[d], here(j))

    def ox_copy(i, j):
        return remote(
            ox.at[rows(j), lanes(i)], ox_in.at[:, lanes(r * hp + i)],
            ox_snd.at[i, j], ox_rcv.at[i, r], half + j,
        )

    def ox_arrival(i, j):
        return remote(
            ox.at[rows(j), lanes(i)], ox_in.at[:, lanes(j * hp + i)],
            ox_snd.at[i, j], ox_rcv.at[i, j], r,
        )

    def lx_copy(j):
        return remote(lx.at[j], lx_in.at[r], lx_snd.at[j], lx_rcv.at[r], half + j)

    def lx_arrival(j):
        return remote(lx.at[j], lx_in.at[j], lx_snd.at[j], lx_rcv.at[j], r)

    others = range(1, half)

    barrier = pltpu.get_barrier_semaphore()
    for step in range(1, n):
        pl.semaphore_signal(
            barrier, inc=1, device_id={"ctx": lax.rem(me + step, n)},
            device_id_type=pl.DeviceIdType.MESH,
        )
    own = [
        pltpu.make_async_copy(lk_far, lk, own_sem.at[3]),
        pltpu.make_async_copy(lv_far, lv, own_sem.at[4]),
        pltpu.make_async_copy(lq_far, lq, own_sem.at[5]),
        pltpu.make_async_copy(sq.at[:, cols(r)], qs.at[rows(r), :], own_sem.at[0]),
        pltpu.make_async_copy(sk.at[:, cols(r)], ks.at[rows(r), :], own_sem.at[1]),
        pltpu.make_async_copy(sv.at[:, cols(r)], vs.at[rows(r), :], own_sem.at[2]),
    ]
    for copy in own:
        copy.start()
    pl.semaphore_wait(barrier, n - 1)

    def spread_head(i, carry):
        for make in (k_copy, v_copy):
            for d in others:
                make(i, d).start()

        @pl.when(upper)
        def _():
            for d in range(half):
                qx_copy(i, d).start()

        for d in others:
            q_copy(i, d).start()
        return carry

    first = (hp + 1) // 2
    lax.fori_loop(0, first, spread_head, 0)

    at_row = lax.broadcasted_iota(jnp.int32, (tokens, tokens), 0)
    at_col = lax.broadcasted_iota(jnp.int32, (tokens, tokens), 1)
    causal = at_row >= at_col
    rst[...] = jnp.dot(
        ld[...], (at_row <= at_col).astype(F32),
        precision=lax.Precision.HIGHEST, preferred_element_type=F32,
    )
    for copy in own[:3]:
        copy.wait()
    ends[...] = jnp.broadcast_to(rst[:, tokens - 1 :], ends.shape)

    def states(h, carry):
        down = jnp.broadcast_to(rst[pl.ds(h, 1), :], (tokens, tokens)).T
        to_end = jnp.exp(down[tokens - 1 :, :] - down)
        scaled = (lk[:, lanes(h)].astype(F32) * to_end).astype(BF16)
        st[h] = contract(scaled, lv[:, lanes(h)], ((0,), (0,))).astype(BF16)
        return carry

    lax.fori_loop(0, heads, states, 0, unroll=4)
    for d in others:
        en_copy(d).start()
        st_copy(d).start()
    lax.fori_loop(first, hp, spread_head, 0)

    def within(h, carry):
        across = jnp.broadcast_to(rst[pl.ds(h, 1), :], (tokens, tokens))
        spread = jnp.where(causal, across.T - across, 0.0)
        scores = contract(lq[:, lanes(h)], lk[:, lanes(h)], ((1,), (1,)))
        decayed = jnp.where(causal, jnp.exp(spread) * scores, 0.0).astype(BF16)
        inside[:, lanes(h)] = contract(decayed, lv[:, lanes(h)], ((1,), (0,)))
        return carry


    def attend(query, keys, values, block):
        scores = contract(query, keys, ((1,), (1,)))
        if block is not None:
            row = lax.broadcasted_iota(jnp.int32, scores.shape, 0) + block * tokens
            col = lax.broadcasted_iota(jnp.int32, scores.shape, 1)
            scores = jnp.where(col <= row, scores, MASKED)
        peak = jnp.max(scores, axis=1, keepdims=True) * SCORE_SCALE
        expo = jnp.exp2(scores * SCORE_SCALE - peak)
        mass = jnp.sum(expo, axis=1, keepdims=True)
        result = contract(expo.astype(BF16), values, ((1,), (0,))) * (1.0 / mass)
        level = jnp.broadcast_to(peak + jnp.log2(mass), (tokens, tokens)).T
        return result.astype(BF16), level[0:1, :]

    def head_step(i, carry):
        for d in others:
            k_copy(i, d).wait_recv()
            v_copy(i, d).wait_recv()

        @pl.when(lower)
        def _():
            for d in range(half):
                qx_copy(i, d).wait_recv()
            for b in range(half):
                result, level = attend(
                    qx[rows(b), lanes(i)], ks[:, lanes(i)], vs[:, lanes(i)], None
                )
                ox[rows(b), lanes(i)] = result
                lx[b, pl.ds(i, 1), :] = level
            for b in range(half):
                ox_copy(i, b).start()

        for d in others:
            q_copy(i, d).wait_recv()
        for b in range(half):
            upto = (b + 1) * tokens
            result, level = attend(
                qs[rows(b), lanes(i)], ks[:upto, lanes(i)], vs[:upto, lanes(i)], b
            )
            os[rows(b), lanes(i)] = result
            ls[b, pl.ds(i, 1), :] = level
        for d in others:
            os_copy(i, d).start()
        return carry

    def priors():
        for d in others:
            en_copy(d).wait_recv()
            st_copy(d).wait_recv()

        st_in[r] = st[pl.ds(r * hp, hp)]
        ends_in[r] = ends[...]

        def one(i, carry):
            state = jnp.where(upper, tot_in[i].astype(F32), 0.0)
            for c in range(half):
                pr[c, i] = state.astype(BF16)
                keep = jnp.exp(ends_in[c, pl.ds(r * hp + i, 1), :])
                state = keep * state + st_in[c, i].astype(F32)
            tot[i] = state.astype(BF16)
            return carry

        lax.fori_loop(0, hp, one, 0, unroll=2)

    for copy in own[3:]:
        copy.wait()

    lax.fori_loop(0, first, head_step, 0)

    @pl.when(lower)
    def _():
        tot_in[...] = jnp.zeros_like(tot_in)
        priors()
        tot_copy().start()
        for d in others:
            pr_copy(d).start()

    lax.fori_loop(first, hp, head_step, 0)

    @pl.when(lower)
    def _():
        for b in range(half):
            lx_copy(b).start()

    for d in others:
        ls_copy(d).start()

    @pl.when(upper)
    def _():
        tot_copy().wait_recv()
        priors()
        for d in others:
            pr_copy(d).start()

    lax.fori_loop(0, heads, within, 0, unroll=4)
    pr_in[r] = pr[r]
    os_in[:, cols(r)] = os[rows(r), :]
    ls_in[r] = ls[r]

    for d in others:
        pr_copy(d).wait_recv()

    def finish(j, carry):
        def head(i, inner):
            h = j * hp + i
            down = jnp.broadcast_to(rst[pl.ds(h, 1), :], (tokens, tokens)).T
            scaled = (lq[:, lanes(h)].astype(F32) * jnp.exp(down)).astype(BF16)
            total = inside[:, lanes(h)] + contract(scaled, pr_in[j, i], ((1,), (0,)))
            norm = lax.rsqrt(jnp.mean(total * total, axis=1, keepdims=True) + NORM_EPS)
            lin_out[:, lanes(h)] = (total * norm).astype(BF16)
            return inner

        return lax.fori_loop(0, hp, head, carry, unroll=True)

    lax.fori_loop(0, half, finish, 0)

    for d in others:
        for i in range(hp):
            os_arrival(i, d).wait_recv()
        ls_copy(d).wait_recv()

    @pl.when(lower)
    def _():
        soft_out[...] = os_in[...]

    @pl.when(upper)
    def _():
        for j in range(half):
            lx_arrival(j).wait_recv()
            for i in range(hp):
                ox_arrival(i, j).wait_recv()

        def merge(j, carry):
            def head(i, inner):
                h = j * hp + i
                gap = lx_in[j, pl.ds(i, 1), :] - ls_in[j, pl.ds(i, 1), :]
                gap = jnp.broadcast_to(gap, (tokens, tokens)).T
                near = 1.0 / (1.0 + jnp.exp2(gap))
                far = 1.0 / (1.0 + jnp.exp2(-gap))
                mixed = near * os_in[:, lanes(h)].astype(F32)
                mixed = mixed + far * ox_in[:, lanes(h)].astype(F32)
                soft_out[:, lanes(h)] = mixed.astype(BF16)
                return inner

            return lax.fori_loop(0, hp, head, carry, unroll=True)

        lax.fori_loop(0, half, merge, 0)

    for make in (en_copy, st_copy, pr_copy, ls_copy):
        for d in others:
            make(d).wait_send()
    for make in (k_copy, v_copy, q_copy, os_copy):
        for i in range(hp):
            for d in others:
                make(i, d).wait_send()

    @pl.when(upper)
    def _():
        for i in range(hp):
            for d in range(half):
                qx_copy(i, d).wait_send()

    @pl.when(lower)
    def _():
        tot_copy().wait_send()
        for j in range(half):
            lx_copy(j).wait_send()
            for i in range(hp):
                ox_copy(i, j).wait_send()


norm_eps = 1e-06
masked_score = -1e30
key_span = 512
query_span = 512


def entering(value, axis, join, neutral):
    count, mine = (lax.axis_size(axis), lax.axis_index(axis))
    pieces = jax.tree.map(lambda part: lax.all_gather(part, axis), value)
    subtotal = jax.tree.map(
        lambda part, zero: jnp.full_like(part, 0) + jnp.asarray(zero, part.dtype), value, neutral
    )

    def step(position, subtotal):
        longer = join(subtotal, jax.tree.map(lambda part: part[position], pieces))
        return jax.tree.map(lambda new, old: jnp.where(position < mine, new, old), longer, subtotal)

    return lax.fori_loop(0, count - 1, step, subtotal)


def merge_states(earlier, later):
    decay_early, state_early = earlier
    decay_late, state_late = later
    return (decay_early * decay_late, decay_late[:, None, None] * state_early + state_late)


def lightning_core(lin_query, lin_key, lin_value, log_decay):
    tokens = lin_query.shape[0]
    heads_here = log_decay.shape[1]
    query_heads = lin_query.reshape(tokens, heads_here, HEAD_DIM)
    key_heads = lin_key.reshape(tokens, heads_here, HEAD_DIM)
    value_heads = lin_value.reshape(tokens, heads_here, HEAD_DIM)
    running_sum = jnp.cumsum(log_decay, axis=0)
    ending = running_sum[-1]
    scores = jnp.einsum("thd,shd->hts", query_heads, key_heads, preferred_element_type=jnp.float32)
    causal = jnp.arange(tokens)[:, None] >= jnp.arange(tokens)[None, :]
    spread = running_sum.T[:, :, None] - running_sum.T[:, None, :]
    decayed = (
        jnp.where(causal[None], jnp.exp(jnp.where(causal[None], spread, 0.0)), 0.0) * scores
    ).astype(jnp.bfloat16)
    inside = jnp.einsum("hts,shd->thd", decayed, value_heads, preferred_element_type=jnp.float32)
    to_end = jnp.exp(ending[None, :] - running_sum)
    key_scaled = (key_heads.astype(jnp.float32) * to_end[:, :, None]).astype(jnp.bfloat16)
    block_state = jnp.einsum(
        "shd,she->hde", key_scaled, value_heads, preferred_element_type=jnp.float32
    )
    block_decay = jnp.exp(ending)
    before = entering(
        (block_decay, block_state),
        "ctx",
        merge_states,
        (jnp.ones_like(block_decay), jnp.zeros_like(block_state)),
    )
    prior_state = before[1]
    query_scaled = (query_heads.astype(jnp.float32) * jnp.exp(running_sum)[:, :, None]).astype(
        jnp.bfloat16
    )
    outside = jnp.einsum(
        "thd,hde->the",
        query_scaled,
        prior_state.astype(jnp.bfloat16),
        preferred_element_type=jnp.float32,
    )
    total = inside + outside
    normed = total * lax.rsqrt(jnp.mean(total * total, axis=-1, keepdims=True) + norm_eps)
    return normed.reshape(tokens, heads_here * HEAD_DIM).astype(jnp.bfloat16)


def prepare_queries(query_mine, tokens, quarter, head_slot):
    rows_all = query_mine.shape[0]
    heads_now = query_mine.shape[1] // HEAD_DIM
    tile_rows = query_span if rows_all % query_span == 0 else rows_all
    blocks_count = rows_all // tile_rows
    query_blocks = query_mine.reshape(blocks_count, tile_rows, heads_now, HEAD_DIM)
    index_all = jnp.arange(rows_all, dtype=jnp.int32)
    token_slots = index_all // quarter * tokens + head_slot * quarter + index_all % quarter
    initial = (
        jnp.full((blocks_count, tile_rows, heads_now), masked_score, jnp.float32),
        jnp.zeros((blocks_count, tile_rows, heads_now), jnp.float32),
        jnp.zeros((blocks_count, tile_rows, heads_now, HEAD_DIM), jnp.float32),
    )
    return (query_blocks, token_slots.reshape(blocks_count, tile_rows), initial)


def attend_keys(carry, query_blocks, query_places, keys_flat, values_flat, key_places):
    key_total = keys_flat.shape[0]
    heads_now = query_blocks.shape[2]
    keys_heads = keys_flat.reshape(key_total, heads_now, HEAD_DIM)
    values_heads = values_flat.reshape(key_total, heads_now, HEAD_DIM)
    score_scale = HEAD_DIM ** (-0.5)

    def per_block(packed):
        best_start, mass_start, accum_start, query_tile, query_where = packed
        latest_query = jnp.max(query_where)

        def per_span(span_index, running):
            start_row = span_index * key_span
            key_where = lax.dynamic_slice_in_dim(key_places, start_row, key_span, 0)

            def compute(state_now):
                best_now, mass_now, accum_now = state_now
                key_tile = lax.dynamic_slice_in_dim(keys_heads, start_row, key_span, 0)
                value_tile = lax.dynamic_slice_in_dim(values_heads, start_row, key_span, 0)
                scores = (
                    jnp.einsum(
                        "qhd,khd->qhk", query_tile, key_tile, preferred_element_type=jnp.float32
                    )
                    * score_scale
                )
                allowed = (key_where[None, :] <= query_where[:, None])[:, None, :]
                scores = jnp.where(allowed, scores, masked_score)
                best_next = jnp.maximum(best_now, jnp.max(scores, axis=-1))
                expo = jnp.where(allowed, jnp.exp(scores - best_next[:, :, None]), 0.0)
                shrink = jnp.exp(best_now - best_next)
                mass_next = mass_now * shrink + jnp.sum(expo, axis=-1)
                accum_next = accum_now * shrink[:, :, None] + jnp.einsum(
                    "qhk,khd->qhd",
                    expo.astype(jnp.bfloat16),
                    value_tile,
                    preferred_element_type=jnp.float32,
                )
                return (best_next, mass_next, accum_next)

            def unchanged(state_now):
                return state_now

            return lax.cond(jnp.min(key_where) <= latest_query, compute, unchanged, running)

        return lax.fori_loop(
            0, key_total // key_span, per_span, (best_start, mass_start, accum_start)
        )

    return lax.map(per_block, (carry[0], carry[1], carry[2], query_blocks, query_places))


def softmax_core(soft_query, soft_key, soft_value):
    tokens = soft_query.shape[0]
    quarter = tokens // lax.axis_size("head")
    head_slot = lax.axis_index("head")
    query_moved, key_moved, value_moved = (
        lax.all_to_all(soft_query, "head", split_axis=0, concat_axis=1, tiled=True),
        lax.all_to_all(soft_key, "head", split_axis=0, concat_axis=1, tiled=True),
        lax.all_to_all(soft_value, "head", split_axis=0, concat_axis=1, tiled=True),
    )
    query_mine, key_mine, value_mine = (
        lax.all_to_all(query_moved, "ctx", split_axis=1, concat_axis=0, tiled=True),
        lax.all_to_all(key_moved, "ctx", split_axis=1, concat_axis=0, tiled=True),
        lax.all_to_all(value_moved, "ctx", split_axis=1, concat_axis=0, tiled=True),
    )
    query_blocks, query_places, initial = prepare_queries(query_mine, tokens, quarter, head_slot)
    resident_rows = key_mine.shape[0]
    pieces = (
        lax.all_gather(key_mine, "head", axis=0, tiled=True),
        lax.all_gather(value_mine, "head", axis=0, tiled=True),
    )
    key_total = pieces[0].shape[0]
    index_all = jnp.arange(key_total, dtype=jnp.int32)
    source = index_all // resident_rows
    within = index_all % resident_rows
    token_slots = within // quarter * tokens + source * quarter + within % quarter
    result = attend_keys(initial, query_blocks, query_places, pieces[0], pieces[1], token_slots)
    best_final, mass_final, accum_final = result
    outcome = (
        (accum_final / mass_final[..., None]).reshape(query_mine.shape[0], -1).astype(jnp.bfloat16)
    )
    return lax.all_to_all(
        lax.all_to_all(outcome, "ctx", split_axis=0, concat_axis=1, tiled=True),
        "head",
        split_axis=1,
        concat_axis=0,
        tiled=True,
    )


def plain_shards(lin_query, lin_key, lin_value, log_decay, soft_query, soft_key, soft_value):
    lin_out = lightning_core(lin_query, lin_key, lin_value, log_decay)
    soft_out = softmax_core(soft_query, soft_key, soft_value)
    return (lin_out, soft_out)


def shards(lin_query, lin_key, lin_value, log_decay, soft_query, soft_key, soft_value):
    n = lax.axis_size("ctx")
    tokens, columns = lin_query.shape
    heads = log_decay.shape[1]
    half = n // 2
    hp = heads // half
    width = hp * HEAD_DIM
    level_rows = -(-hp // 8) * 8
    vmem = pl.BlockSpec(memory_space=pltpu.VMEM)
    far = pl.BlockSpec(memory_space=pltpu.HBM)
    big = pltpu.VMEM((half * tokens, width), BF16)
    full = pltpu.VMEM((tokens, columns), BF16)
    level = pltpu.VMEM((half, level_rows, tokens), F32)
    grid_states = pltpu.VMEM((half, hp, HEAD_DIM, HEAD_DIM), BF16)
    some_states = pltpu.VMEM((hp, HEAD_DIM, HEAD_DIM), BF16)
    dma = pltpu.SemaphoreType.DMA
    ring = [dma((half,)), dma((half,))]
    square = [dma((hp, half)), dma((hp, half))]
    single = [dma, dma]
    return pl.pallas_call(
        functools.partial(kernel, n),
        out_shape=[jax.ShapeDtypeStruct((tokens, columns), BF16)] * 2,
        in_specs=[far] * 3 + [vmem] + [far] * 3,
        out_specs=[vmem] * 2,
        scratch_shapes=[full] * 3 + [big] * 6 + [full] * 2 + [level] * 4
        + [
            pltpu.VMEM((heads, HEAD_DIM, HEAD_DIM), BF16),
            grid_states,
            pltpu.VMEM((heads, tokens), F32),
            pltpu.VMEM((half, heads, tokens), F32),
            grid_states,
            grid_states,
            some_states,
            some_states,
            pltpu.VMEM((heads, tokens), F32),
            pltpu.VMEM((tokens, columns), F32),
            dma((6,)),
        ]
        + square * 4 + ring * 2 + single + ring + square + ring + square + ring,
        compiler_params=pltpu.CompilerParams(
            collective_id=0, has_side_effects=True, vmem_limit_bytes=60 * 1024 * 1024
        ),
        cost_estimate=pl.CostEstimate(
            flops=3 * 10**9, bytes_accessed=4 * 10**6, transcendentals=3 * 10**6
        ),
    )(lin_query, lin_key, lin_value, log_decay.T, soft_query, soft_key, soft_value)


def solution(mesh):
    spec = P("ctx", "head")
    n = mesh.shape["ctx"]

    def body(*args):
        heads = args[3].shape[1]
        if n % 2 or n < 4 or heads % (n // 2):
            return plain_shards(*args)
        return shards(*args)

    return jax.shard_map(
        body, mesh=mesh, in_specs=(spec,) * 7, out_specs=(spec,) * 2, check_vma=False
    )
```

```python
import functools

import jax
import jax.numpy as jnp
from jax import lax
from jax.experimental import pallas as pl
from jax.experimental.pallas import tpu as pltpu
from jax.sharding import PartitionSpec as P

HEAD_DIM = 128
NORM_EPS = 1e-06
MASKED = -1e30
SCORE_SCALE = HEAD_DIM ** (-0.5) * 1.4426950408889634
F32 = jnp.float32
BF16 = jnp.bfloat16


def contract(a, b, dims):
    return lax.dot_general(a, b, (dims, ((), ())), preferred_element_type=F32)


def lanes(index):
    return pl.ds(pl.multiple_of(index * HEAD_DIM, HEAD_DIM), HEAD_DIM)


def kernel(
    n,
    lq_far, lk_far, lv_far, ld, sq, sk, sv,
    both_out,
    lq, lk, lv, qs, ks, vs, qx, os, ox, os_in, ox_in, ls, lx, ls_in, lx_in,
    st, st_in, ends, ends_in, pr, pr_in, tot, tot_in, rst, inside,
    own_sem,
    q_snd, q_rcv, k_snd, k_rcv, v_snd, v_rcv,
    qx_snd, qx_rcv, st_snd, st_rcv, en_snd, en_rcv, tot_snd, tot_rcv,
    pr_snd, pr_rcv, os_snd, os_rcv, ls_snd, ls_rcv, ox_snd, ox_rcv, lx_snd, lx_rcv,
):
    tokens = lq.shape[0]
    heads = ld.shape[0]
    lin_out, soft_out = both_out.at[0], both_out.at[1]
    half = n // 2
    hp = heads // half
    me = lax.axis_index("ctx")
    side = me // half
    r = lax.rem(me, half)
    lower = side == 0
    upper = side == 1

    def peer(d):
        return lax.rem(r + d, half)

    def source(d):
        return lax.rem(r + half - d, half)

    def rows(index):
        if isinstance(index, int):
            return pl.ds(index * tokens, tokens)
        return pl.ds(pl.multiple_of(index * tokens, tokens), tokens)

    def remote(src, dst, snd, rcv, target):
        return pltpu.make_async_remote_copy(
            src_ref=src, dst_ref=dst, send_sem=snd, recv_sem=rcv,
            device_id={"ctx": target}, device_id_type=pl.DeviceIdType.MESH,
        )

    def here(index):
        return side * half + index

    def q_copy(i, d):
        j = peer(d)
        return remote(
            sq.at[:, lanes(j * hp + i)], qs.at[i, rows(r)],
            q_snd.at[i, d], q_rcv.at[i, d], here(j),
        )

    def k_copy(i, d):
        j = peer(d)
        return remote(
            sk.at[:, lanes(j * hp + i)], ks.at[i, rows(r)],
            k_snd.at[i, d], k_rcv.at[i, d], here(j),
        )

    def v_copy(i, d):
        j = peer(d)
        return remote(
            sv.at[:, lanes(j * hp + i)], vs.at[i, rows(r)],
            v_snd.at[i, d], v_rcv.at[i, d], here(j),
        )

    def qx_copy(i, d):
        j = peer(d)
        return remote(
            sq.at[:, lanes(j * hp + i)], qx.at[i, rows(r)],
            qx_snd.at[i, d], qx_rcv.at[i, d], j,
        )

    def st_copy(d):
        j = peer(d)
        return remote(
            st.at[pl.ds(j * hp, hp)], st_in.at[r], st_snd.at[d], st_rcv.at[d], here(j)
        )

    def en_copy(d):
        return remote(ends, ends_in.at[r], en_snd.at[d], en_rcv.at[d], here(peer(d)))

    def tot_copy():
        return remote(tot, tot_in, tot_snd, tot_rcv, half + r)

    def pr_copy(d):
        j = peer(d)
        return remote(pr.at[j], pr_in.at[r], pr_snd.at[d], pr_rcv.at[d], here(j))

    def os_copy(i, d):
        j = peer(d)
        return remote(
            os.at[i, rows(j)], os_in.at[r * hp + i],
            os_snd.at[i, d], os_rcv.at[i, d], here(j),
        )

    def os_arrival(i, d):
        j = source(d)
        return remote(
            os.at[i, rows(j)], os_in.at[j * hp + i],
            os_snd.at[i, d], os_rcv.at[i, d], here(j),
        )

    def ls_copy(i, d):
        j = peer(d)
        return remote(
            ls.at[j, i], ls_in.at[r, i], ls_snd.at[i, d], ls_rcv.at[i, d], here(j)
        )

    def ls_arrival(i, d):
        j = source(d)
        return remote(
            ls.at[j, i], ls_in.at[j, i], ls_snd.at[i, d], ls_rcv.at[i, d], here(j)
        )

    def ox_copy(i, j):
        return remote(
            ox.at[i, rows(j)], ox_in.at[r * hp + i],
            ox_snd.at[i, j], ox_rcv.at[i, r], half + j,
        )

    def ox_arrival(i, j):
        return remote(
            ox.at[i, rows(j)], ox_in.at[j * hp + i],
            ox_snd.at[i, j], ox_rcv.at[i, j], r,
        )

    def lx_copy(i, j):
        return remote(
            lx.at[j, i], lx_in.at[r, i], lx_snd.at[i, j], lx_rcv.at[i, r], half + j
        )

    def lx_arrival(i, j):
        return remote(
            lx.at[j, i], lx_in.at[j, i], lx_snd.at[i, j], lx_rcv.at[i, j], r
        )

    others = range(1, half)

    barrier = pltpu.get_barrier_semaphore()
    for step in range(1, n):
        pl.semaphore_signal(
            barrier, inc=1, device_id={"ctx": lax.rem(me + step, n)},
            device_id_type=pl.DeviceIdType.MESH,
        )
    own = [
        pltpu.make_async_copy(lk_far, lk, own_sem.at[0]),
        pltpu.make_async_copy(lv_far, lv, own_sem.at[1]),
        pltpu.make_async_copy(lq_far, lq, own_sem.at[2]),
    ]
    own += [
        pltpu.make_async_copy(
            whole.at[:, lanes(r * hp + i)], kept.at[i, rows(r)], own_sem.at[3 + a * hp + i]
        )
        for a, (whole, kept) in enumerate(((sq, qs), (sk, ks), (sv, vs)))
        for i in range(hp)
    ]
    for copy in own:
        copy.start()
    pl.semaphore_wait(barrier, n - 1)

    def spread_head(i, carry):
        for make in (k_copy, v_copy):
            for d in others:
                make(i, d).start()

        @pl.when(upper)
        def _():
            for d in range(half):
                qx_copy(i, d).start()

        for d in others:
            q_copy(i, d).start()
        return carry

    first = (hp + 1) // 2
    lax.fori_loop(0, first, spread_head, 0)

    at_row = lax.broadcasted_iota(jnp.int32, (tokens, tokens), 0)
    at_col = lax.broadcasted_iota(jnp.int32, (tokens, tokens), 1)
    causal = at_row >= at_col
    rst[...] = jnp.dot(
        ld[...], (at_row <= at_col).astype(F32),
        precision=lax.Precision.HIGHEST, preferred_element_type=F32,
    )
    for copy in own[:3]:
        copy.wait()
    ends[...] = jnp.broadcast_to(rst[:, tokens - 1 :], ends.shape)

    def states(h, carry):
        down = jnp.broadcast_to(rst[pl.ds(h, 1), :], (tokens, tokens)).T
        to_end = jnp.exp(down[tokens - 1 :, :] - down)
        scaled = (lk[:, lanes(h)].astype(F32) * to_end).astype(BF16)
        st[h] = contract(scaled, lv[:, lanes(h)], ((0,), (0,))).astype(BF16)
        return carry

    lax.fori_loop(0, heads, states, 0, unroll=4)
    for d in others:
        en_copy(d).start()
        st_copy(d).start()
    lax.fori_loop(first, hp, spread_head, 0)

    def within(h, carry):
        across = jnp.broadcast_to(rst[pl.ds(h, 1), :], (tokens, tokens))
        spread = jnp.where(causal, across.T - across, 0.0)
        scores = contract(lq[:, lanes(h)], lk[:, lanes(h)], ((1,), (1,)))
        decayed = jnp.where(causal, jnp.exp(spread) * scores, 0.0).astype(BF16)
        inside[:, lanes(h)] = contract(decayed, lv[:, lanes(h)], ((1,), (0,)))
        return carry


    def attend(query, keys, values, block):
        scores = contract(query, keys, ((1,), (1,)))
        if block is not None:
            row = lax.broadcasted_iota(jnp.int32, scores.shape, 0) + block * tokens
            col = lax.broadcasted_iota(jnp.int32, scores.shape, 1)
            scores = jnp.where(col <= row, scores, MASKED)
        peak = jnp.max(scores, axis=1, keepdims=True) * SCORE_SCALE
        expo = jnp.exp2(scores * SCORE_SCALE - peak)
        mass = jnp.sum(expo, axis=1, keepdims=True)
        result = contract(expo.astype(BF16), values, ((1,), (0,))) * (1.0 / mass)
        level = jnp.broadcast_to(peak + jnp.log2(mass), (tokens, tokens)).T
        return result.astype(BF16), level[0:8, :]

    def head_step(i, carry):
        for d in others:
            k_copy(i, d).wait_recv()
            v_copy(i, d).wait_recv()

        @pl.when(lower)
        def _():
            for d in range(half):
                qx_copy(i, d).wait_recv()
            for b in range(half):
                result, level = attend(
                    qx[i, rows(b)], ks[i], vs[i], None
                )
                ox[i, rows(b)] = result
                lx[b, i] = level
            for b in range(half):
                ox_copy(i, b).start()
                lx_copy(i, b).start()

        for d in others:
            q_copy(i, d).wait_recv()
        for b in range(half):
            upto = (b + 1) * tokens
            result, level = attend(
                qs[i, rows(b)], ks[i, :upto], vs[i, :upto], b
            )
            os[i, rows(b)] = result
            ls[b, i] = level
        for d in others:
            os_copy(i, d).start()
            ls_copy(i, d).start()
        return carry

    def priors():
        for d in others:
            en_copy(d).wait_recv()
            st_copy(d).wait_recv()

        st_in[r] = st[pl.ds(r * hp, hp)]
        ends_in[r] = ends[...]

        def one(i, carry):
            state = jnp.where(upper, tot_in[i].astype(F32), 0.0)
            for c in range(half):
                pr[c, i] = state.astype(BF16)
                keep = jnp.exp(ends_in[c, pl.ds(r * hp + i, 1), :])
                state = keep * state + st_in[c, i].astype(F32)
            tot[i] = state.astype(BF16)
            return carry

        lax.fori_loop(0, hp, one, 0, unroll=2)

    for copy in own[3:]:
        copy.wait()

    lax.fori_loop(0, first, head_step, 0)

    @pl.when(lower)
    def _():
        tot_in[...] = jnp.zeros_like(tot_in)
        priors()
        tot_copy().start()
        for d in others:
            pr_copy(d).start()

    lax.fori_loop(first, hp, head_step, 0)

    @pl.when(upper)
    def _():
        tot_copy().wait_recv()
        priors()
        for d in others:
            pr_copy(d).start()

    lax.fori_loop(0, heads, within, 0, unroll=4)
    pr_in[r] = pr[r]
    os_in[pl.ds(r * hp, hp)] = os[:, rows(r), :]
    ls_in[r] = ls[r]

    for d in others:
        pr_copy(d).wait_recv()

    def finish(j, carry):
        def head(i, inner):
            h = j * hp + i
            down = jnp.broadcast_to(rst[pl.ds(h, 1), :], (tokens, tokens)).T
            scaled = (lq[:, lanes(h)].astype(F32) * jnp.exp(down)).astype(BF16)
            total = inside[:, lanes(h)] + contract(scaled, pr_in[j, i], ((1,), (0,)))
            norm = lax.rsqrt(jnp.mean(total * total, axis=1, keepdims=True) + NORM_EPS)
            lin_out[:, lanes(h)] = (total * norm).astype(BF16)
            return inner

        return lax.fori_loop(0, hp, head, carry, unroll=True)

    lax.fori_loop(0, half, finish, 0)

    def arrive(i, carry):
        for d in others:
            os_arrival(i, d).wait_recv()
            ls_arrival(i, d).wait_recv()

        @pl.when(lower)
        def _():
            for j in range(half):
                soft_out[:, lanes(j * hp + i)] = os_in[j * hp + i]

        @pl.when(upper)
        def _():
            for j in range(half):
                lx_arrival(i, j).wait_recv()
                ox_arrival(i, j).wait_recv()
            for j in range(half):
                h = j * hp + i
                gap = lx_in[j, i, 0:1, :] - ls_in[j, i, 0:1, :]
                gap = jnp.broadcast_to(gap, (tokens, tokens)).T
                near = 1.0 / (1.0 + jnp.exp2(gap))
                far = 1.0 / (1.0 + jnp.exp2(-gap))
                mixed = near * os_in[h].astype(F32) + far * ox_in[h].astype(F32)
                soft_out[:, lanes(h)] = mixed.astype(BF16)

        return carry

    lax.fori_loop(0, hp, arrive, 0)

    for make in (en_copy, st_copy, pr_copy):
        for d in others:
            make(d).wait_send()
    for make in (k_copy, v_copy, q_copy, os_copy, ls_copy):
        for i in range(hp):
            for d in others:
                make(i, d).wait_send()

    @pl.when(upper)
    def _():
        for i in range(hp):
            for d in range(half):
                qx_copy(i, d).wait_send()

    @pl.when(lower)
    def _():
        tot_copy().wait_send()
        for j in range(half):
            for i in range(hp):
                lx_copy(i, j).wait_send()
                ox_copy(i, j).wait_send()


norm_eps = 1e-06
masked_score = -1e30
key_span = 512
query_span = 512


def entering(value, axis, join, neutral):
    count, mine = (lax.axis_size(axis), lax.axis_index(axis))
    pieces = jax.tree.map(lambda part: lax.all_gather(part, axis), value)
    subtotal = jax.tree.map(
        lambda part, zero: jnp.full_like(part, 0) + jnp.asarray(zero, part.dtype), value, neutral
    )

    def step(position, subtotal):
        longer = join(subtotal, jax.tree.map(lambda part: part[position], pieces))
        return jax.tree.map(lambda new, old: jnp.where(position < mine, new, old), longer, subtotal)

    return lax.fori_loop(0, count - 1, step, subtotal)


def merge_states(earlier, later):
    decay_early, state_early = earlier
    decay_late, state_late = later
    return (decay_early * decay_late, decay_late[:, None, None] * state_early + state_late)


def lightning_core(lin_query, lin_key, lin_value, log_decay):
    tokens = lin_query.shape[0]
    heads_here = log_decay.shape[1]
    query_heads = lin_query.reshape(tokens, heads_here, HEAD_DIM)
    key_heads = lin_key.reshape(tokens, heads_here, HEAD_DIM)
    value_heads = lin_value.reshape(tokens, heads_here, HEAD_DIM)
    running_sum = jnp.cumsum(log_decay, axis=0)
    ending = running_sum[-1]
    scores = jnp.einsum("thd,shd->hts", query_heads, key_heads, preferred_element_type=jnp.float32)
    causal = jnp.arange(tokens)[:, None] >= jnp.arange(tokens)[None, :]
    spread = running_sum.T[:, :, None] - running_sum.T[:, None, :]
    decayed = (
        jnp.where(causal[None], jnp.exp(jnp.where(causal[None], spread, 0.0)), 0.0) * scores
    ).astype(jnp.bfloat16)
    inside = jnp.einsum("hts,shd->thd", decayed, value_heads, preferred_element_type=jnp.float32)
    to_end = jnp.exp(ending[None, :] - running_sum)
    key_scaled = (key_heads.astype(jnp.float32) * to_end[:, :, None]).astype(jnp.bfloat16)
    block_state = jnp.einsum(
        "shd,she->hde", key_scaled, value_heads, preferred_element_type=jnp.float32
    )
    block_decay = jnp.exp(ending)
    before = entering(
        (block_decay, block_state),
        "ctx",
        merge_states,
        (jnp.ones_like(block_decay), jnp.zeros_like(block_state)),
    )
    prior_state = before[1]
    query_scaled = (query_heads.astype(jnp.float32) * jnp.exp(running_sum)[:, :, None]).astype(
        jnp.bfloat16
    )
    outside = jnp.einsum(
        "thd,hde->the",
        query_scaled,
        prior_state.astype(jnp.bfloat16),
        preferred_element_type=jnp.float32,
    )
    total = inside + outside
    normed = total * lax.rsqrt(jnp.mean(total * total, axis=-1, keepdims=True) + norm_eps)
    return normed.reshape(tokens, heads_here * HEAD_DIM).astype(jnp.bfloat16)


def prepare_queries(query_mine, tokens, quarter, head_slot):
    rows_all = query_mine.shape[0]
    heads_now = query_mine.shape[1] // HEAD_DIM
    tile_rows = query_span if rows_all % query_span == 0 else rows_all
    blocks_count = rows_all // tile_rows
    query_blocks = query_mine.reshape(blocks_count, tile_rows, heads_now, HEAD_DIM)
    index_all = jnp.arange(rows_all, dtype=jnp.int32)
    token_slots = index_all // quarter * tokens + head_slot * quarter + index_all % quarter
    initial = (
        jnp.full((blocks_count, tile_rows, heads_now), masked_score, jnp.float32),
        jnp.zeros((blocks_count, tile_rows, heads_now), jnp.float32),
        jnp.zeros((blocks_count, tile_rows, heads_now, HEAD_DIM), jnp.float32),
    )
    return (query_blocks, token_slots.reshape(blocks_count, tile_rows), initial)


def attend_keys(carry, query_blocks, query_places, keys_flat, values_flat, key_places):
    key_total = keys_flat.shape[0]
    heads_now = query_blocks.shape[2]
    keys_heads = keys_flat.reshape(key_total, heads_now, HEAD_DIM)
    values_heads = values_flat.reshape(key_total, heads_now, HEAD_DIM)
    score_scale = HEAD_DIM ** (-0.5)

    def per_block(packed):
        best_start, mass_start, accum_start, query_tile, query_where = packed
        latest_query = jnp.max(query_where)

        def per_span(span_index, running):
            start_row = span_index * key_span
            key_where = lax.dynamic_slice_in_dim(key_places, start_row, key_span, 0)

            def compute(state_now):
                best_now, mass_now, accum_now = state_now
                key_tile = lax.dynamic_slice_in_dim(keys_heads, start_row, key_span, 0)
                value_tile = lax.dynamic_slice_in_dim(values_heads, start_row, key_span, 0)
                scores = (
                    jnp.einsum(
                        "qhd,khd->qhk", query_tile, key_tile, preferred_element_type=jnp.float32
                    )
                    * score_scale
                )
                allowed = (key_where[None, :] <= query_where[:, None])[:, None, :]
                scores = jnp.where(allowed, scores, masked_score)
                best_next = jnp.maximum(best_now, jnp.max(scores, axis=-1))
                expo = jnp.where(allowed, jnp.exp(scores - best_next[:, :, None]), 0.0)
                shrink = jnp.exp(best_now - best_next)
                mass_next = mass_now * shrink + jnp.sum(expo, axis=-1)
                accum_next = accum_now * shrink[:, :, None] + jnp.einsum(
                    "qhk,khd->qhd",
                    expo.astype(jnp.bfloat16),
                    value_tile,
                    preferred_element_type=jnp.float32,
                )
                return (best_next, mass_next, accum_next)

            def unchanged(state_now):
                return state_now

            return lax.cond(jnp.min(key_where) <= latest_query, compute, unchanged, running)

        return lax.fori_loop(
            0, key_total // key_span, per_span, (best_start, mass_start, accum_start)
        )

    return lax.map(per_block, (carry[0], carry[1], carry[2], query_blocks, query_places))


def softmax_core(soft_query, soft_key, soft_value):
    tokens = soft_query.shape[0]
    quarter = tokens // lax.axis_size("head")
    head_slot = lax.axis_index("head")
    query_moved, key_moved, value_moved = (
        lax.all_to_all(soft_query, "head", split_axis=0, concat_axis=1, tiled=True),
        lax.all_to_all(soft_key, "head", split_axis=0, concat_axis=1, tiled=True),
        lax.all_to_all(soft_value, "head", split_axis=0, concat_axis=1, tiled=True),
    )
    query_mine, key_mine, value_mine = (
        lax.all_to_all(query_moved, "ctx", split_axis=1, concat_axis=0, tiled=True),
        lax.all_to_all(key_moved, "ctx", split_axis=1, concat_axis=0, tiled=True),
        lax.all_to_all(value_moved, "ctx", split_axis=1, concat_axis=0, tiled=True),
    )
    query_blocks, query_places, initial = prepare_queries(query_mine, tokens, quarter, head_slot)
    resident_rows = key_mine.shape[0]
    pieces = (
        lax.all_gather(key_mine, "head", axis=0, tiled=True),
        lax.all_gather(value_mine, "head", axis=0, tiled=True),
    )
    key_total = pieces[0].shape[0]
    index_all = jnp.arange(key_total, dtype=jnp.int32)
    source = index_all // resident_rows
    within = index_all % resident_rows
    token_slots = within // quarter * tokens + source * quarter + within % quarter
    result = attend_keys(initial, query_blocks, query_places, pieces[0], pieces[1], token_slots)
    best_final, mass_final, accum_final = result
    outcome = (
        (accum_final / mass_final[..., None]).reshape(query_mine.shape[0], -1).astype(jnp.bfloat16)
    )
    return lax.all_to_all(
        lax.all_to_all(outcome, "ctx", split_axis=0, concat_axis=1, tiled=True),
        "head",
        split_axis=1,
        concat_axis=0,
        tiled=True,
    )


def plain_shards(lin_query, lin_key, lin_value, log_decay, soft_query, soft_key, soft_value):
    lin_out = lightning_core(lin_query, lin_key, lin_value, log_decay)
    soft_out = softmax_core(soft_query, soft_key, soft_value)
    return (lin_out, soft_out)


def shards(lin_query, lin_key, lin_value, log_decay, soft_query, soft_key, soft_value):
    n = lax.axis_size("ctx")
    tokens, columns = lin_query.shape
    heads = log_decay.shape[1]
    half = n // 2
    hp = heads // half
    vmem = pl.BlockSpec(memory_space=pltpu.VMEM)
    far = pl.BlockSpec(memory_space=pltpu.HBM)
    big = pltpu.VMEM((hp, half * tokens, HEAD_DIM), BF16)
    pieces = pltpu.VMEM((heads, tokens, HEAD_DIM), BF16)
    full = pltpu.VMEM((tokens, columns), BF16)
    level = pltpu.VMEM((half, hp, 8, tokens), F32)
    grid_states = pltpu.VMEM((half, hp, HEAD_DIM, HEAD_DIM), BF16)
    some_states = pltpu.VMEM((hp, HEAD_DIM, HEAD_DIM), BF16)
    dma = pltpu.SemaphoreType.DMA
    ring = [dma((half,)), dma((half,))]
    square = [dma((hp, half)), dma((hp, half))]
    single = [dma, dma]
    both = pl.pallas_call(
        functools.partial(kernel, n),
        out_shape=jax.ShapeDtypeStruct((2, tokens, columns), BF16),
        in_specs=[far] * 3 + [vmem] + [far] * 3,
        out_specs=vmem,
        scratch_shapes=[full] * 3 + [big] * 6 + [pieces] * 2 + [level] * 4
        + [
            pltpu.VMEM((heads, HEAD_DIM, HEAD_DIM), BF16),
            grid_states,
            pltpu.VMEM((heads, tokens), F32),
            pltpu.VMEM((half, heads, tokens), F32),
            grid_states,
            grid_states,
            some_states,
            some_states,
            pltpu.VMEM((heads, tokens), F32),
            pltpu.VMEM((tokens, columns), F32),
            dma((3 + 3 * hp,)),
        ]
        + square * 4 + ring * 2 + single + ring + square * 4,
        compiler_params=pltpu.CompilerParams(
            collective_id=0, has_side_effects=True, vmem_limit_bytes=60 * 1024 * 1024
        ),
        cost_estimate=pl.CostEstimate(
            flops=3 * 10**9, bytes_accessed=4 * 10**6, transcendentals=3 * 10**6
        ),
    )(lin_query, lin_key, lin_value, log_decay.T, soft_query, soft_key, soft_value)
    return both[0], both[1]


def solution(mesh):
    spec = P("ctx", "head")
    n = mesh.shape["ctx"]

    def body(*args):
        heads = args[3].shape[1]
        if n % 2 or n < 4 or heads % (n // 2):
            return plain_shards(*args)
        return shards(*args)

    return jax.shard_map(
        body, mesh=mesh, in_specs=(spec,) * 7, out_specs=(spec,) * 2, check_vma=False
    )
```

```python
import functools

import jax
import jax.numpy as jnp
from jax import lax
from jax.experimental import pallas as pl
from jax.experimental.pallas import tpu as pltpu
from jax.sharding import PartitionSpec as P

HEAD_DIM = 128
NORM_EPS = 1e-06
MASKED = -1e30
SCORE_SCALE = HEAD_DIM ** (-0.5) * 1.4426950408889634
F32 = jnp.float32
BF16 = jnp.bfloat16


def contract(a, b, dims):
    return lax.dot_general(a, b, (dims, ((), ())), preferred_element_type=F32)


def lanes(index):
    return pl.ds(pl.multiple_of(index * HEAD_DIM, HEAD_DIM), HEAD_DIM)


def kernel(
    n,
    lq_far, lk_far, lv_far, ld, sq, sk, sv,
    both_out,
    lq, lk, lv, qs, ks, vs, qx, os, ox, os_in, ox_in, ls, lx, ls_in, lx_in,
    st, st_in, ends, ends_in, pr, pr_in, tot, tot_in, rst, inside,
    own_sem,
    q_snd, q_rcv, k_snd, k_rcv, v_snd, v_rcv,
    qx_snd, qx_rcv, st_snd, st_rcv, en_snd, en_rcv, tot_snd, tot_rcv,
    pr_snd, pr_rcv, os_snd, os_rcv, ls_snd, ls_rcv, ox_snd, ox_rcv, lx_snd, lx_rcv,
):
    tokens = lq.shape[0]
    heads = ld.shape[0]
    lin_out, soft_out = both_out.at[0], both_out.at[1]
    half = n // 2
    hp = heads // half
    width = hp * HEAD_DIM
    me = lax.axis_index("ctx")
    side = me // half
    r = lax.rem(me, half)
    lower = side == 0
    pair = me // 2
    spot = lax.rem(me, 2)
    partner = me + 1 - 2 * spot
    pairs = n // 2
    hh = heads // 2
    upper = side == 1

    def peer(d):
        return lax.rem(r + d, half)

    def source(d):
        return lax.rem(r + half - d, half)

    def cols(index):
        return pl.ds(pl.multiple_of(index * width, width), width)

    def rows(index):
        if isinstance(index, int):
            return pl.ds(index * tokens, tokens)
        return pl.ds(pl.multiple_of(index * tokens, tokens), tokens)

    def remote(src, dst, snd, rcv, target):
        return pltpu.make_async_remote_copy(
            src_ref=src, dst_ref=dst, send_sem=snd, recv_sem=rcv,
            device_id={"ctx": target}, device_id_type=pl.DeviceIdType.MESH,
        )

    def here(index):
        return side * half + index

    def q_copy(i, d):
        j = peer(d)
        return remote(
            sq.at[:, lanes(j * hp + i)], qs.at[rows(r), lanes(i)],
            q_snd.at[i, d], q_rcv.at[i, d], here(j),
        )

    def k_copy(i, d):
        j = peer(d)
        return remote(
            sk.at[:, lanes(j * hp + i)], ks.at[rows(r), lanes(i)],
            k_snd.at[i, d], k_rcv.at[i, d], here(j),
        )

    def v_copy(i, d):
        j = peer(d)
        return remote(
            sv.at[:, lanes(j * hp + i)], vs.at[rows(r), lanes(i)],
            v_snd.at[i, d], v_rcv.at[i, d], here(j),
        )

    def qx_copy(i, d):
        j = peer(d)
        return remote(
            sq.at[:, lanes(j * hp + i)], qx.at[rows(r), lanes(i)],
            qx_snd.at[i, d], qx_rcv.at[i, d], j,
        )

    def st_copy():
        return remote(st.at[pl.ds((1 - spot) * hh, hh)], st_in, st_snd, st_rcv, partner)

    def en_copy():
        return remote(ends, ends_in, en_snd, en_rcv, partner)

    def tot_copy():
        return remote(tot, tot_in, tot_snd, tot_rcv, lax.rem(me + 2, n))

    def pr_copy():
        return remote(pr, pr_in.at[pl.ds(spot * hh, hh)], pr_snd, pr_rcv, partner)

    def pr_arrival():
        return remote(pr, pr_in.at[pl.ds((1 - spot) * hh, hh)], pr_snd, pr_rcv, partner)

    def os_copy(i, d):
        j = peer(d)
        return remote(
            os.at[rows(j), lanes(i)], os_in.at[:, lanes(r * hp + i)],
            os_snd.at[i, d], os_rcv.at[i, d], here(j),
        )

    def os_arrival(i, d):
        j = source(d)
        return remote(
            os.at[rows(j), lanes(i)], os_in.at[:, lanes(j * hp + i)],
            os_snd.at[i, d], os_rcv.at[i, d], here(j),
        )

    def ls_copy(d):
        j = peer(d)
        return remote(ls.at[j], ls_in.at[r], ls_snd.at[d], ls_rcv.at[d], here(j))

    def ox_copy(i, j):
        return remote(
            ox.at[rows(j), lanes(i)], ox_in.at[:, lanes(r * hp + i)],
            ox_snd.at[i, j], ox_rcv.at[i, r], half + j,
        )

    def ox_arrival(i, j):
        return remote(
            ox.at[rows(j), lanes(i)], ox_in.at[:, lanes(j * hp + i)],
            ox_snd.at[i, j], ox_rcv.at[i, j], r,
        )

    def lx_copy(j):
        return remote(lx.at[j], lx_in.at[r], lx_snd.at[j], lx_rcv.at[r], half + j)

    def lx_arrival(j):
        return remote(lx.at[j], lx_in.at[j], lx_snd.at[j], lx_rcv.at[j], r)

    others = range(1, half)

    barrier = pltpu.get_barrier_semaphore()
    for step in range(1, n):
        pl.semaphore_signal(
            barrier, inc=1, device_id={"ctx": lax.rem(me + step, n)},
            device_id_type=pl.DeviceIdType.MESH,
        )
    own = [
        pltpu.make_async_copy(lk_far, lk, own_sem.at[3]),
        pltpu.make_async_copy(lv_far, lv, own_sem.at[4]),
        pltpu.make_async_copy(lq_far, lq, own_sem.at[5]),
        pltpu.make_async_copy(sq.at[:, cols(r)], qs.at[rows(r), :], own_sem.at[0]),
        pltpu.make_async_copy(sk.at[:, cols(r)], ks.at[rows(r), :], own_sem.at[1]),
        pltpu.make_async_copy(sv.at[:, cols(r)], vs.at[rows(r), :], own_sem.at[2]),
    ]
    for copy in own:
        copy.start()
    pl.semaphore_wait(barrier, n - 1)

    def spread_head(i, carry):
        for make in (k_copy, v_copy):
            for d in others:
                make(i, d).start()

        @pl.when(upper)
        def _():
            for d in range(half):
                qx_copy(i, d).start()

        for d in others:
            q_copy(i, d).start()
        return carry

    first = (hp + 1) // 2
    lax.fori_loop(0, first, spread_head, 0)

    at_row = lax.broadcasted_iota(jnp.int32, (tokens, tokens), 0)
    at_col = lax.broadcasted_iota(jnp.int32, (tokens, tokens), 1)
    causal = at_row >= at_col
    rst[...] = jnp.dot(
        ld[...], (at_row <= at_col).astype(F32),
        precision=lax.Precision.HIGHEST, preferred_element_type=F32,
    )
    for copy in own[:3]:
        copy.wait()
    ends[...] = jnp.broadcast_to(rst[:, tokens - 1 :], ends.shape)

    def states(h, carry):
        down = jnp.broadcast_to(rst[pl.ds(h, 1), :], (tokens, tokens)).T
        to_end = jnp.exp(down[tokens - 1 :, :] - down)
        scaled = (lk[:, lanes(h)].astype(F32) * to_end).astype(BF16)
        st[h] = contract(scaled, lv[:, lanes(h)], ((0,), (0,))).astype(BF16)
        return carry

    lax.fori_loop(0, heads, states, 0, unroll=4)
    en_copy().start()
    st_copy().start()
    lax.fori_loop(first, hp, spread_head, 0)

    def within(h, carry):
        across = jnp.broadcast_to(rst[pl.ds(h, 1), :], (tokens, tokens))
        spread = jnp.where(causal, across.T - across, 0.0)
        scores = contract(lq[:, lanes(h)], lk[:, lanes(h)], ((1,), (1,)))
        decayed = jnp.where(causal, jnp.exp(spread) * scores, 0.0).astype(BF16)
        inside[:, lanes(h)] = contract(decayed, lv[:, lanes(h)], ((1,), (0,)))
        return carry


    def attend(query, keys, values, block):
        scores = contract(query, keys, ((1,), (1,)))
        if block is not None:
            row = lax.broadcasted_iota(jnp.int32, scores.shape, 0) + block * tokens
            col = lax.broadcasted_iota(jnp.int32, scores.shape, 1)
            scores = jnp.where(col <= row, scores, MASKED)
        peak = jnp.max(scores, axis=1, keepdims=True) * SCORE_SCALE
        expo = jnp.exp2(scores * SCORE_SCALE - peak)
        mass = jnp.sum(expo, axis=1, keepdims=True)
        result = contract(expo.astype(BF16), values, ((1,), (0,))) * (1.0 / mass)
        level = jnp.broadcast_to(peak + jnp.log2(mass), (tokens, tokens)).T
        return result.astype(BF16), level[0:1, :]

    def priors():
        en_copy().wait_recv()
        st_copy().wait_recv()

        @pl.when(pair > 0)
        def _():
            tot_copy().wait_recv()

        @pl.when(pair == 0)
        def _():
            tot_in[...] = jnp.zeros_like(tot_in)

        first_here = spot == 0

        def one(i, carry):
            h = spot * hh + i
            enter = tot_in[i].astype(F32)
            mine = st[h].astype(F32)
            theirs = st_in[i].astype(F32)
            keep_mine = jnp.exp(ends[pl.ds(h, 1), :])
            keep_theirs = jnp.exp(ends_in[pl.ds(h, 1), :])
            early = jnp.where(first_here, mine, theirs)
            late = jnp.where(first_here, theirs, mine)
            middle = jnp.where(first_here, keep_mine, keep_theirs) * enter + early
            leave = jnp.where(first_here, keep_theirs, keep_mine) * middle + late
            tot[i] = leave.astype(BF16)
            pr[i] = jnp.where(first_here, middle, enter).astype(BF16)
            pr_in[h] = jnp.where(first_here, enter, middle).astype(BF16)
            return carry

        lax.fori_loop(0, hh, one, 0, unroll=2)

        @pl.when(pair < pairs - 1)
        def _():
            tot_copy().start()

        pr_copy().start()

    def head_step(i, carry):
        for d in others:
            k_copy(i, d).wait_recv()
            v_copy(i, d).wait_recv()

        @pl.when(lower)
        def _():
            for d in range(half):
                qx_copy(i, d).wait_recv()
            for b in range(half):
                result, level = attend(
                    qx[rows(b), lanes(i)], ks[:, lanes(i)], vs[:, lanes(i)], None
                )
                ox[rows(b), lanes(i)] = result
                lx[b, pl.ds(i, 1), :] = level
            for b in range(half):
                ox_copy(i, b).start()

        for d in others:
            q_copy(i, d).wait_recv()
        for b in range(half):
            upto = (b + 1) * tokens
            result, level = attend(
                qs[rows(b), lanes(i)], ks[:upto, lanes(i)], vs[:upto, lanes(i)], b
            )
            os[rows(b), lanes(i)] = result
            ls[b, pl.ds(i, 1), :] = level
        for d in others:
            os_copy(i, d).start()

        @pl.when(i == jnp.minimum(pair, hp - 1))
        def _():
            priors()

        return carry

    for copy in own[3:]:
        copy.wait()

    lax.fori_loop(0, hp, head_step, 0)

    @pl.when(lower)
    def _():
        for b in range(half):
            lx_copy(b).start()

    for d in others:
        ls_copy(d).start()

    lax.fori_loop(0, heads, within, 0, unroll=4)
    os_in[:, cols(r)] = os[rows(r), :]
    ls_in[r] = ls[r]

    pr_arrival().wait_recv()

    def finish(j, carry):
        def head(i, inner):
            h = j * hp + i
            down = jnp.broadcast_to(rst[pl.ds(h, 1), :], (tokens, tokens)).T
            scaled = (lq[:, lanes(h)].astype(F32) * jnp.exp(down)).astype(BF16)
            total = inside[:, lanes(h)] + contract(scaled, pr_in[h], ((1,), (0,)))
            norm = lax.rsqrt(jnp.mean(total * total, axis=1, keepdims=True) + NORM_EPS)
            lin_out[:, lanes(h)] = (total * norm).astype(BF16)
            return inner

        return lax.fori_loop(0, hp, head, carry, unroll=True)

    lax.fori_loop(0, half, finish, 0)

    for d in others:
        for i in range(hp):
            os_arrival(i, d).wait_recv()
        ls_copy(d).wait_recv()

    @pl.when(lower)
    def _():
        soft_out[...] = os_in[...]

    @pl.when(upper)
    def _():
        for j in range(half):
            lx_arrival(j).wait_recv()
            for i in range(hp):
                ox_arrival(i, j).wait_recv()

        def merge(j, carry):
            def head(i, inner):
                h = j * hp + i
                gap = lx_in[j, pl.ds(i, 1), :] - ls_in[j, pl.ds(i, 1), :]
                gap = jnp.broadcast_to(gap, (tokens, tokens)).T
                near = 1.0 / (1.0 + jnp.exp2(gap))
                far = 1.0 / (1.0 + jnp.exp2(-gap))
                mixed = near * os_in[:, lanes(h)].astype(F32)
                mixed = mixed + far * ox_in[:, lanes(h)].astype(F32)
                soft_out[:, lanes(h)] = mixed.astype(BF16)
                return inner

            return lax.fori_loop(0, hp, head, carry, unroll=True)

        lax.fori_loop(0, half, merge, 0)

    for make in (en_copy, st_copy, pr_copy):
        make().wait_send()
    for d in others:
        ls_copy(d).wait_send()

    @pl.when(pair < pairs - 1)
    def _():
        tot_copy().wait_send()

    for make in (k_copy, v_copy, q_copy, os_copy):
        for i in range(hp):
            for d in others:
                make(i, d).wait_send()

    @pl.when(upper)
    def _():
        for i in range(hp):
            for d in range(half):
                qx_copy(i, d).wait_send()

    @pl.when(lower)
    def _():
        for j in range(half):
            lx_copy(j).wait_send()
            for i in range(hp):
                ox_copy(i, j).wait_send()


norm_eps = 1e-06
masked_score = -1e30
key_span = 512
query_span = 512


def entering(value, axis, join, neutral):
    count, mine = (lax.axis_size(axis), lax.axis_index(axis))
    pieces = jax.tree.map(lambda part: lax.all_gather(part, axis), value)
    subtotal = jax.tree.map(
        lambda part, zero: jnp.full_like(part, 0) + jnp.asarray(zero, part.dtype), value, neutral
    )

    def step(position, subtotal):
        longer = join(subtotal, jax.tree.map(lambda part: part[position], pieces))
        return jax.tree.map(lambda new, old: jnp.where(position < mine, new, old), longer, subtotal)

    return lax.fori_loop(0, count - 1, step, subtotal)


def merge_states(earlier, later):
    decay_early, state_early = earlier
    decay_late, state_late = later
    return (decay_early * decay_late, decay_late[:, None, None] * state_early + state_late)


def lightning_core(lin_query, lin_key, lin_value, log_decay):
    tokens = lin_query.shape[0]
    heads_here = log_decay.shape[1]
    query_heads = lin_query.reshape(tokens, heads_here, HEAD_DIM)
    key_heads = lin_key.reshape(tokens, heads_here, HEAD_DIM)
    value_heads = lin_value.reshape(tokens, heads_here, HEAD_DIM)
    running_sum = jnp.cumsum(log_decay, axis=0)
    ending = running_sum[-1]
    scores = jnp.einsum("thd,shd->hts", query_heads, key_heads, preferred_element_type=jnp.float32)
    causal = jnp.arange(tokens)[:, None] >= jnp.arange(tokens)[None, :]
    spread = running_sum.T[:, :, None] - running_sum.T[:, None, :]
    decayed = (
        jnp.where(causal[None], jnp.exp(jnp.where(causal[None], spread, 0.0)), 0.0) * scores
    ).astype(jnp.bfloat16)
    inside = jnp.einsum("hts,shd->thd", decayed, value_heads, preferred_element_type=jnp.float32)
    to_end = jnp.exp(ending[None, :] - running_sum)
    key_scaled = (key_heads.astype(jnp.float32) * to_end[:, :, None]).astype(jnp.bfloat16)
    block_state = jnp.einsum(
        "shd,she->hde", key_scaled, value_heads, preferred_element_type=jnp.float32
    )
    block_decay = jnp.exp(ending)
    before = entering(
        (block_decay, block_state),
        "ctx",
        merge_states,
        (jnp.ones_like(block_decay), jnp.zeros_like(block_state)),
    )
    prior_state = before[1]
    query_scaled = (query_heads.astype(jnp.float32) * jnp.exp(running_sum)[:, :, None]).astype(
        jnp.bfloat16
    )
    outside = jnp.einsum(
        "thd,hde->the",
        query_scaled,
        prior_state.astype(jnp.bfloat16),
        preferred_element_type=jnp.float32,
    )
    total = inside + outside
    normed = total * lax.rsqrt(jnp.mean(total * total, axis=-1, keepdims=True) + norm_eps)
    return normed.reshape(tokens, heads_here * HEAD_DIM).astype(jnp.bfloat16)


def prepare_queries(query_mine, tokens, quarter, head_slot):
    rows_all = query_mine.shape[0]
    heads_now = query_mine.shape[1] // HEAD_DIM
    tile_rows = query_span if rows_all % query_span == 0 else rows_all
    blocks_count = rows_all // tile_rows
    query_blocks = query_mine.reshape(blocks_count, tile_rows, heads_now, HEAD_DIM)
    index_all = jnp.arange(rows_all, dtype=jnp.int32)
    token_slots = index_all // quarter * tokens + head_slot * quarter + index_all % quarter
    initial = (
        jnp.full((blocks_count, tile_rows, heads_now), masked_score, jnp.float32),
        jnp.zeros((blocks_count, tile_rows, heads_now), jnp.float32),
        jnp.zeros((blocks_count, tile_rows, heads_now, HEAD_DIM), jnp.float32),
    )
    return (query_blocks, token_slots.reshape(blocks_count, tile_rows), initial)


def attend_keys(carry, query_blocks, query_places, keys_flat, values_flat, key_places):
    key_total = keys_flat.shape[0]
    heads_now = query_blocks.shape[2]
    keys_heads = keys_flat.reshape(key_total, heads_now, HEAD_DIM)
    values_heads = values_flat.reshape(key_total, heads_now, HEAD_DIM)
    score_scale = HEAD_DIM ** (-0.5)

    def per_block(packed):
        best_start, mass_start, accum_start, query_tile, query_where = packed
        latest_query = jnp.max(query_where)

        def per_span(span_index, running):
            start_row = span_index * key_span
            key_where = lax.dynamic_slice_in_dim(key_places, start_row, key_span, 0)

            def compute(state_now):
                best_now, mass_now, accum_now = state_now
                key_tile = lax.dynamic_slice_in_dim(keys_heads, start_row, key_span, 0)
                value_tile = lax.dynamic_slice_in_dim(values_heads, start_row, key_span, 0)
                scores = (
                    jnp.einsum(
                        "qhd,khd->qhk", query_tile, key_tile, preferred_element_type=jnp.float32
                    )
                    * score_scale
                )
                allowed = (key_where[None, :] <= query_where[:, None])[:, None, :]
                scores = jnp.where(allowed, scores, masked_score)
                best_next = jnp.maximum(best_now, jnp.max(scores, axis=-1))
                expo = jnp.where(allowed, jnp.exp(scores - best_next[:, :, None]), 0.0)
                shrink = jnp.exp(best_now - best_next)
                mass_next = mass_now * shrink + jnp.sum(expo, axis=-1)
                accum_next = accum_now * shrink[:, :, None] + jnp.einsum(
                    "qhk,khd->qhd",
                    expo.astype(jnp.bfloat16),
                    value_tile,
                    preferred_element_type=jnp.float32,
                )
                return (best_next, mass_next, accum_next)

            def unchanged(state_now):
                return state_now

            return lax.cond(jnp.min(key_where) <= latest_query, compute, unchanged, running)

        return lax.fori_loop(
            0, key_total // key_span, per_span, (best_start, mass_start, accum_start)
        )

    return lax.map(per_block, (carry[0], carry[1], carry[2], query_blocks, query_places))


def softmax_core(soft_query, soft_key, soft_value):
    tokens = soft_query.shape[0]
    quarter = tokens // lax.axis_size("head")
    head_slot = lax.axis_index("head")
    query_moved, key_moved, value_moved = (
        lax.all_to_all(soft_query, "head", split_axis=0, concat_axis=1, tiled=True),
        lax.all_to_all(soft_key, "head", split_axis=0, concat_axis=1, tiled=True),
        lax.all_to_all(soft_value, "head", split_axis=0, concat_axis=1, tiled=True),
    )
    query_mine, key_mine, value_mine = (
        lax.all_to_all(query_moved, "ctx", split_axis=1, concat_axis=0, tiled=True),
        lax.all_to_all(key_moved, "ctx", split_axis=1, concat_axis=0, tiled=True),
        lax.all_to_all(value_moved, "ctx", split_axis=1, concat_axis=0, tiled=True),
    )
    query_blocks, query_places, initial = prepare_queries(query_mine, tokens, quarter, head_slot)
    resident_rows = key_mine.shape[0]
    pieces = (
        lax.all_gather(key_mine, "head", axis=0, tiled=True),
        lax.all_gather(value_mine, "head", axis=0, tiled=True),
    )
    key_total = pieces[0].shape[0]
    index_all = jnp.arange(key_total, dtype=jnp.int32)
    source = index_all // resident_rows
    within = index_all % resident_rows
    token_slots = within // quarter * tokens + source * quarter + within % quarter
    result = attend_keys(initial, query_blocks, query_places, pieces[0], pieces[1], token_slots)
    best_final, mass_final, accum_final = result
    outcome = (
        (accum_final / mass_final[..., None]).reshape(query_mine.shape[0], -1).astype(jnp.bfloat16)
    )
    return lax.all_to_all(
        lax.all_to_all(outcome, "ctx", split_axis=0, concat_axis=1, tiled=True),
        "head",
        split_axis=1,
        concat_axis=0,
        tiled=True,
    )


def plain_shards(lin_query, lin_key, lin_value, log_decay, soft_query, soft_key, soft_value):
    lin_out = lightning_core(lin_query, lin_key, lin_value, log_decay)
    soft_out = softmax_core(soft_query, soft_key, soft_value)
    return (lin_out, soft_out)


def shards(lin_query, lin_key, lin_value, log_decay, soft_query, soft_key, soft_value):
    n = lax.axis_size("ctx")
    tokens, columns = lin_query.shape
    heads = log_decay.shape[1]
    half = n // 2
    hp = heads // half
    width = hp * HEAD_DIM
    level_rows = -(-hp // 8) * 8
    vmem = pl.BlockSpec(memory_space=pltpu.VMEM)
    far = pl.BlockSpec(memory_space=pltpu.HBM)
    big = pltpu.VMEM((half * tokens, width), BF16)
    full = pltpu.VMEM((tokens, columns), BF16)
    level = pltpu.VMEM((half, level_rows, tokens), F32)
    some_states = pltpu.VMEM((heads // 2, HEAD_DIM, HEAD_DIM), BF16)
    dma = pltpu.SemaphoreType.DMA
    ring = [dma((half,)), dma((half,))]
    square = [dma((hp, half)), dma((hp, half))]
    single = [dma, dma]
    both = pl.pallas_call(
        functools.partial(kernel, n),
        out_shape=jax.ShapeDtypeStruct((2, tokens, columns), BF16),
        in_specs=[far] * 3 + [vmem] + [far] * 3,
        out_specs=vmem,
        scratch_shapes=[full] * 3 + [big] * 6 + [full] * 2 + [level] * 4
        + [
            pltpu.VMEM((heads, HEAD_DIM, HEAD_DIM), BF16),
            some_states,
            pltpu.VMEM((heads, tokens), F32),
            pltpu.VMEM((heads, tokens), F32),
            some_states,
            pltpu.VMEM((heads, HEAD_DIM, HEAD_DIM), BF16),
            some_states,
            some_states,
            pltpu.VMEM((heads, tokens), F32),
            pltpu.VMEM((tokens, columns), F32),
            dma((6,)),
        ]
        + square * 4 + single * 4 + square + ring + square + ring,
        compiler_params=pltpu.CompilerParams(
            collective_id=0, has_side_effects=True, vmem_limit_bytes=60 * 1024 * 1024
        ),
        cost_estimate=pl.CostEstimate(
            flops=3 * 10**9, bytes_accessed=4 * 10**6, transcendentals=3 * 10**6
        ),
    )(lin_query, lin_key, lin_value, log_decay.T, soft_query, soft_key, soft_value)
    return both[0], both[1]


def solution(mesh):
    spec = P("ctx", "head")
    n = mesh.shape["ctx"]

    def body(*args):
        heads = args[3].shape[1]
        if n % 2 or n < 4 or heads % (n // 2):
            return plain_shards(*args)
        return shards(*args)

    return jax.shard_map(
        body, mesh=mesh, in_specs=(spec,) * 7, out_specs=(spec,) * 2, check_vma=False
    )
```

```python
import functools

import jax
import jax.numpy as jnp
from jax import lax
from jax.experimental import pallas as pl
from jax.experimental.pallas import tpu as pltpu
from jax.sharding import PartitionSpec as P

HEAD_DIM = 128
NORM_EPS = 1e-06
MASKED = -1e30
SCORE_SCALE = HEAD_DIM ** (-0.5) * 1.4426950408889634
F32 = jnp.float32
BF16 = jnp.bfloat16


def contract(a, b, dims):
    return lax.dot_general(a, b, (dims, ((), ())), preferred_element_type=F32)


def lanes(index):
    return pl.ds(pl.multiple_of(index * HEAD_DIM, HEAD_DIM), HEAD_DIM)


def kernel(
    n,
    lq_far, lk_far, lv_far, ld, sq, sk, sv,
    both_out,
    lq, lk, lv, qs, ks, vs, qx, os, ox, os_in, ox_in, ls, lx, ls_in, lx_in,
    st, st_in, ends, ends_in, pr, pr_in, tot, tot_in, rst, inside,
    own_sem,
    q_snd, q_rcv, k_snd, k_rcv, v_snd, v_rcv,
    qx_snd, qx_rcv, st_snd, st_rcv, en_snd, en_rcv, tot_snd, tot_rcv,
    pr_snd, pr_rcv, os_snd, os_rcv, ls_snd, ls_rcv, ox_snd, ox_rcv, lx_snd, lx_rcv,
):
    tokens = lq.shape[0]
    heads = ld.shape[0]
    lin_out, soft_out = both_out.at[0], both_out.at[1]
    half = n // 2
    hp = heads // half
    width = hp * HEAD_DIM
    me = lax.axis_index("ctx")
    side = me // half
    r = lax.rem(me, half)
    lower = side == 0
    pair = me // 2
    spot = lax.rem(me, 2)
    partner = me + 1 - 2 * spot
    pairs = n // 2
    hh = heads // 2
    upper = side == 1

    def peer(d):
        return lax.rem(r + d, half)

    def source(d):
        return lax.rem(r + half - d, half)

    def cols(index):
        return pl.ds(pl.multiple_of(index * width, width), width)

    def rows(index):
        if isinstance(index, int):
            return pl.ds(index * tokens, tokens)
        return pl.ds(pl.multiple_of(index * tokens, tokens), tokens)

    def remote(src, dst, snd, rcv, target):
        return pltpu.make_async_remote_copy(
            src_ref=src, dst_ref=dst, send_sem=snd, recv_sem=rcv,
            device_id={"ctx": target}, device_id_type=pl.DeviceIdType.MESH,
        )

    def here(index):
        return side * half + index

    def q_copy(i, d):
        j = peer(d)
        return remote(
            sq.at[:, lanes(j * hp + i)], qs.at[rows(r), lanes(i)],
            q_snd.at[i, d], q_rcv.at[i, d], here(j),
        )

    def k_copy(i, d):
        j = peer(d)
        return remote(
            sk.at[:, lanes(j * hp + i)], ks.at[rows(r), lanes(i)],
            k_snd.at[i, d], k_rcv.at[i, d], here(j),
        )

    def v_copy(i, d):
        j = peer(d)
        return remote(
            sv.at[:, lanes(j * hp + i)], vs.at[rows(r), lanes(i)],
            v_snd.at[i, d], v_rcv.at[i, d], here(j),
        )

    def qx_copy(i, d):
        j = peer(d)
        return remote(
            sq.at[:, lanes(j * hp + i)], qx.at[rows(r), lanes(i)],
            qx_snd.at[i, d], qx_rcv.at[i, d], j,
        )

    def st_copy():
        return remote(st.at[pl.ds((1 - spot) * hh, hh)], st_in, st_snd, st_rcv, partner)

    def en_copy():
        return remote(ends, ends_in, en_snd, en_rcv, partner)

    def tot_copy():
        return remote(tot, tot_in, tot_snd, tot_rcv, lax.rem(me + 2, n))

    def pr_copy():
        return remote(pr, pr_in.at[pl.ds(spot * hh, hh)], pr_snd, pr_rcv, partner)

    def pr_arrival():
        return remote(pr, pr_in.at[pl.ds((1 - spot) * hh, hh)], pr_snd, pr_rcv, partner)

    def os_copy(i, d):
        j = peer(d)
        return remote(
            os.at[rows(j), lanes(i)], os_in.at[:, lanes(r * hp + i)],
            os_snd.at[i, d], os_rcv.at[i, d], here(j),
        )

    def os_arrival(i, d):
        j = source(d)
        return remote(
            os.at[rows(j), lanes(i)], os_in.at[:, lanes(j * hp + i)],
            os_snd.at[i, d], os_rcv.at[i, d], here(j),
        )

    def ls_copy(d):
        j = peer(d)
        return remote(ls.at[j], ls_in.at[r], ls_snd.at[d], ls_rcv.at[d], here(j))

    def ox_copy(i, j):
        return remote(
            ox.at[rows(j), lanes(i)], ox_in.at[:, lanes(r * hp + i)],
            ox_snd.at[i, j], ox_rcv.at[i, r], half + j,
        )

    def ox_arrival(i, j):
        return remote(
            ox.at[rows(j), lanes(i)], ox_in.at[:, lanes(j * hp + i)],
            ox_snd.at[i, j], ox_rcv.at[i, j], r,
        )

    def lx_copy(j):
        return remote(lx.at[j], lx_in.at[r], lx_snd.at[j], lx_rcv.at[r], half + j)

    def lx_arrival(j):
        return remote(lx.at[j], lx_in.at[j], lx_snd.at[j], lx_rcv.at[j], r)

    others = range(1, half)

    barrier = pltpu.get_barrier_semaphore()
    for step in range(1, n):
        pl.semaphore_signal(
            barrier, inc=1, device_id={"ctx": lax.rem(me + step, n)},
            device_id_type=pl.DeviceIdType.MESH,
        )
    own = [
        pltpu.make_async_copy(lk_far, lk, own_sem.at[3]),
        pltpu.make_async_copy(lv_far, lv, own_sem.at[4]),
        pltpu.make_async_copy(lq_far, lq, own_sem.at[5]),
        pltpu.make_async_copy(sq.at[:, cols(r)], qs.at[rows(r), :], own_sem.at[0]),
        pltpu.make_async_copy(sk.at[:, cols(r)], ks.at[rows(r), :], own_sem.at[1]),
        pltpu.make_async_copy(sv.at[:, cols(r)], vs.at[rows(r), :], own_sem.at[2]),
    ]
    for copy in own:
        copy.start()
    pl.semaphore_wait(barrier, n - 1)

    def spread_head(i, carry):
        for make in (k_copy, v_copy):
            for d in others:
                make(i, d).start()

        @pl.when(upper)
        def _():
            for d in range(half):
                qx_copy(i, d).start()

        for d in others:
            q_copy(i, d).start()
        return carry

    first = (hp + 1) // 2
    lax.fori_loop(0, first, spread_head, 0)

    at_row = lax.broadcasted_iota(jnp.int32, (tokens, tokens), 0)
    at_col = lax.broadcasted_iota(jnp.int32, (tokens, tokens), 1)
    causal = at_row >= at_col
    rst[...] = jnp.dot(
        ld[...], (at_row <= at_col).astype(F32),
        precision=lax.Precision.HIGHEST, preferred_element_type=F32,
    )
    for copy in own[:3]:
        copy.wait()
    ends[...] = jnp.broadcast_to(rst[:, tokens - 1 :], ends.shape)

    def states(h, carry):
        down = jnp.broadcast_to(rst[pl.ds(h, 1), :], (tokens, tokens)).T
        to_end = jnp.exp(down[tokens - 1 :, :] - down)
        scaled = (lk[:, lanes(h)].astype(F32) * to_end).astype(BF16)
        st[h] = contract(scaled, lv[:, lanes(h)], ((0,), (0,))).astype(BF16)
        return carry

    lax.fori_loop(0, heads, states, 0, unroll=4)
    en_copy().start()
    st_copy().start()
    lax.fori_loop(first, hp, spread_head, 0)

    def within(h, carry):
        across = jnp.broadcast_to(rst[pl.ds(h, 1), :], (tokens, tokens))
        spread = jnp.where(causal, across.T - across, 0.0)
        scores = contract(lq[:, lanes(h)], lk[:, lanes(h)], ((1,), (1,)))
        decayed = jnp.where(causal, jnp.exp(spread) * scores, 0.0).astype(BF16)
        inside[:, lanes(h)] = contract(decayed, lv[:, lanes(h)], ((1,), (0,)))
        return carry


    def attend(query, keys, values, block):
        scores = contract(query, keys, ((1,), (1,)))
        if block is not None:
            row = lax.broadcasted_iota(jnp.int32, scores.shape, 0) + block * tokens
            col = lax.broadcasted_iota(jnp.int32, scores.shape, 1)
            scores = jnp.where(col <= row, scores, MASKED)
        peak = jnp.max(scores, axis=1, keepdims=True) * SCORE_SCALE
        expo = jnp.exp2(scores * SCORE_SCALE - peak)
        mass = jnp.sum(expo, axis=1, keepdims=True)
        result = contract(expo.astype(BF16), values, ((1,), (0,))) * (1.0 / mass)
        level = jnp.broadcast_to(peak + jnp.log2(mass), (tokens, tokens)).T
        return result.astype(BF16), level[0:1, :]

    def priors():
        en_copy().wait_recv()
        st_copy().wait_recv()

        @pl.when(pair > 0)
        def _():
            tot_copy().wait_recv()

        @pl.when(pair == 0)
        def _():
            tot_in[...] = jnp.zeros_like(tot_in)

        first_here = spot == 0

        def one(i, carry):
            h = spot * hh + i
            enter = tot_in[i].astype(F32)
            mine = st[h].astype(F32)
            theirs = st_in[i].astype(F32)
            keep_mine = jnp.exp(ends[pl.ds(h, 1), :])
            keep_theirs = jnp.exp(ends_in[pl.ds(h, 1), :])
            early = jnp.where(first_here, mine, theirs)
            late = jnp.where(first_here, theirs, mine)
            middle = jnp.where(first_here, keep_mine, keep_theirs) * enter + early
            leave = jnp.where(first_here, keep_theirs, keep_mine) * middle + late
            tot[i] = leave.astype(BF16)
            pr[i] = jnp.where(first_here, middle, enter).astype(BF16)
            pr_in[h] = jnp.where(first_here, enter, middle).astype(BF16)
            return carry

        lax.fori_loop(0, hh, one, 0, unroll=2)

        @pl.when(pair < pairs - 1)
        def _():
            tot_copy().start()

        pr_copy().start()

    def head_step(i, carry):
        @pl.when(i == jnp.minimum(pair, hp - 1))
        def _():
            priors()

        for d in others:
            k_copy(i, d).wait_recv()
            v_copy(i, d).wait_recv()

        @pl.when(lower)
        def _():
            for d in range(half):
                qx_copy(i, d).wait_recv()
            for b in range(half):
                result, level = attend(
                    qx[rows(b), lanes(i)], ks[:, lanes(i)], vs[:, lanes(i)], None
                )
                ox[rows(b), lanes(i)] = result
                lx[b, pl.ds(i, 1), :] = level
            for b in range(half):
                ox_copy(i, b).start()

        for d in others:
            q_copy(i, d).wait_recv()
        for b in range(half):
            upto = (b + 1) * tokens
            result, level = attend(
                qs[rows(b), lanes(i)], ks[:upto, lanes(i)], vs[:upto, lanes(i)], b
            )
            os[rows(b), lanes(i)] = result
            ls[b, pl.ds(i, 1), :] = level
        for d in others:
            os_copy(i, d).start()

        return carry

    for copy in own[3:]:
        copy.wait()

    lax.fori_loop(0, hp, head_step, 0)

    @pl.when(lower)
    def _():
        for b in range(half):
            lx_copy(b).start()

    for d in others:
        ls_copy(d).start()

    lax.fori_loop(0, heads, within, 0, unroll=4)
    os_in[:, cols(r)] = os[rows(r), :]
    ls_in[r] = ls[r]

    pr_arrival().wait_recv()

    def finish(j, carry):
        def head(i, inner):
            h = j * hp + i
            down = jnp.broadcast_to(rst[pl.ds(h, 1), :], (tokens, tokens)).T
            scaled = (lq[:, lanes(h)].astype(F32) * jnp.exp(down)).astype(BF16)
            total = inside[:, lanes(h)] + contract(scaled, pr_in[h], ((1,), (0,)))
            norm = lax.rsqrt(jnp.mean(total * total, axis=1, keepdims=True) + NORM_EPS)
            lin_out[:, lanes(h)] = (total * norm).astype(BF16)
            return inner

        return lax.fori_loop(0, hp, head, carry, unroll=True)

    lax.fori_loop(0, half, finish, 0)

    for d in others:
        for i in range(hp):
            os_arrival(i, d).wait_recv()
        ls_copy(d).wait_recv()

    @pl.when(lower)
    def _():
        soft_out[...] = os_in[...]

    @pl.when(upper)
    def _():
        for j in range(half):
            lx_arrival(j).wait_recv()
            for i in range(hp):
                ox_arrival(i, j).wait_recv()

        def merge(j, carry):
            def head(i, inner):
                h = j * hp + i
                gap = lx_in[j, pl.ds(i, 1), :] - ls_in[j, pl.ds(i, 1), :]
                gap = jnp.broadcast_to(gap, (tokens, tokens)).T
                near = 1.0 / (1.0 + jnp.exp2(gap))
                far = 1.0 / (1.0 + jnp.exp2(-gap))
                mixed = near * os_in[:, lanes(h)].astype(F32)
                mixed = mixed + far * ox_in[:, lanes(h)].astype(F32)
                soft_out[:, lanes(h)] = mixed.astype(BF16)
                return inner

            return lax.fori_loop(0, hp, head, carry, unroll=True)

        lax.fori_loop(0, half, merge, 0)

    for make in (en_copy, st_copy, pr_copy):
        make().wait_send()
    for d in others:
        ls_copy(d).wait_send()

    @pl.when(pair < pairs - 1)
    def _():
        tot_copy().wait_send()

    for make in (k_copy, v_copy, q_copy, os_copy):
        for i in range(hp):
            for d in others:
                make(i, d).wait_send()

    @pl.when(upper)
    def _():
        for i in range(hp):
            for d in range(half):
                qx_copy(i, d).wait_send()

    @pl.when(lower)
    def _():
        for j in range(half):
            lx_copy(j).wait_send()
            for i in range(hp):
                ox_copy(i, j).wait_send()


norm_eps = 1e-06
masked_score = -1e30
key_span = 512
query_span = 512


def entering(value, axis, join, neutral):
    count, mine = (lax.axis_size(axis), lax.axis_index(axis))
    pieces = jax.tree.map(lambda part: lax.all_gather(part, axis), value)
    subtotal = jax.tree.map(
        lambda part, zero: jnp.full_like(part, 0) + jnp.asarray(zero, part.dtype), value, neutral
    )

    def step(position, subtotal):
        longer = join(subtotal, jax.tree.map(lambda part: part[position], pieces))
        return jax.tree.map(lambda new, old: jnp.where(position < mine, new, old), longer, subtotal)

    return lax.fori_loop(0, count - 1, step, subtotal)


def merge_states(earlier, later):
    decay_early, state_early = earlier
    decay_late, state_late = later
    return (decay_early * decay_late, decay_late[:, None, None] * state_early + state_late)


def lightning_core(lin_query, lin_key, lin_value, log_decay):
    tokens = lin_query.shape[0]
    heads_here = log_decay.shape[1]
    query_heads = lin_query.reshape(tokens, heads_here, HEAD_DIM)
    key_heads = lin_key.reshape(tokens, heads_here, HEAD_DIM)
    value_heads = lin_value.reshape(tokens, heads_here, HEAD_DIM)
    running_sum = jnp.cumsum(log_decay, axis=0)
    ending = running_sum[-1]
    scores = jnp.einsum("thd,shd->hts", query_heads, key_heads, preferred_element_type=jnp.float32)
    causal = jnp.arange(tokens)[:, None] >= jnp.arange(tokens)[None, :]
    spread = running_sum.T[:, :, None] - running_sum.T[:, None, :]
    decayed = (
        jnp.where(causal[None], jnp.exp(jnp.where(causal[None], spread, 0.0)), 0.0) * scores
    ).astype(jnp.bfloat16)
    inside = jnp.einsum("hts,shd->thd", decayed, value_heads, preferred_element_type=jnp.float32)
    to_end = jnp.exp(ending[None, :] - running_sum)
    key_scaled = (key_heads.astype(jnp.float32) * to_end[:, :, None]).astype(jnp.bfloat16)
    block_state = jnp.einsum(
        "shd,she->hde", key_scaled, value_heads, preferred_element_type=jnp.float32
    )
    block_decay = jnp.exp(ending)
    before = entering(
        (block_decay, block_state),
        "ctx",
        merge_states,
        (jnp.ones_like(block_decay), jnp.zeros_like(block_state)),
    )
    prior_state = before[1]
    query_scaled = (query_heads.astype(jnp.float32) * jnp.exp(running_sum)[:, :, None]).astype(
        jnp.bfloat16
    )
    outside = jnp.einsum(
        "thd,hde->the",
        query_scaled,
        prior_state.astype(jnp.bfloat16),
        preferred_element_type=jnp.float32,
    )
    total = inside + outside
    normed = total * lax.rsqrt(jnp.mean(total * total, axis=-1, keepdims=True) + norm_eps)
    return normed.reshape(tokens, heads_here * HEAD_DIM).astype(jnp.bfloat16)


def prepare_queries(query_mine, tokens, quarter, head_slot):
    rows_all = query_mine.shape[0]
    heads_now = query_mine.shape[1] // HEAD_DIM
    tile_rows = query_span if rows_all % query_span == 0 else rows_all
    blocks_count = rows_all // tile_rows
    query_blocks = query_mine.reshape(blocks_count, tile_rows, heads_now, HEAD_DIM)
    index_all = jnp.arange(rows_all, dtype=jnp.int32)
    token_slots = index_all // quarter * tokens + head_slot * quarter + index_all % quarter
    initial = (
        jnp.full((blocks_count, tile_rows, heads_now), masked_score, jnp.float32),
        jnp.zeros((blocks_count, tile_rows, heads_now), jnp.float32),
        jnp.zeros((blocks_count, tile_rows, heads_now, HEAD_DIM), jnp.float32),
    )
    return (query_blocks, token_slots.reshape(blocks_count, tile_rows), initial)


def attend_keys(carry, query_blocks, query_places, keys_flat, values_flat, key_places):
    key_total = keys_flat.shape[0]
    heads_now = query_blocks.shape[2]
    keys_heads = keys_flat.reshape(key_total, heads_now, HEAD_DIM)
    values_heads = values_flat.reshape(key_total, heads_now, HEAD_DIM)
    score_scale = HEAD_DIM ** (-0.5)

    def per_block(packed):
        best_start, mass_start, accum_start, query_tile, query_where = packed
        latest_query = jnp.max(query_where)

        def per_span(span_index, running):
            start_row = span_index * key_span
            key_where = lax.dynamic_slice_in_dim(key_places, start_row, key_span, 0)

            def compute(state_now):
                best_now, mass_now, accum_now = state_now
                key_tile = lax.dynamic_slice_in_dim(keys_heads, start_row, key_span, 0)
                value_tile = lax.dynamic_slice_in_dim(values_heads, start_row, key_span, 0)
                scores = (
                    jnp.einsum(
                        "qhd,khd->qhk", query_tile, key_tile, preferred_element_type=jnp.float32
                    )
                    * score_scale
                )
                allowed = (key_where[None, :] <= query_where[:, None])[:, None, :]
                scores = jnp.where(allowed, scores, masked_score)
                best_next = jnp.maximum(best_now, jnp.max(scores, axis=-1))
                expo = jnp.where(allowed, jnp.exp(scores - best_next[:, :, None]), 0.0)
                shrink = jnp.exp(best_now - best_next)
                mass_next = mass_now * shrink + jnp.sum(expo, axis=-1)
                accum_next = accum_now * shrink[:, :, None] + jnp.einsum(
                    "qhk,khd->qhd",
                    expo.astype(jnp.bfloat16),
                    value_tile,
                    preferred_element_type=jnp.float32,
                )
                return (best_next, mass_next, accum_next)

            def unchanged(state_now):
                return state_now

            return lax.cond(jnp.min(key_where) <= latest_query, compute, unchanged, running)

        return lax.fori_loop(
            0, key_total // key_span, per_span, (best_start, mass_start, accum_start)
        )

    return lax.map(per_block, (carry[0], carry[1], carry[2], query_blocks, query_places))


def softmax_core(soft_query, soft_key, soft_value):
    tokens = soft_query.shape[0]
    quarter = tokens // lax.axis_size("head")
    head_slot = lax.axis_index("head")
    query_moved, key_moved, value_moved = (
        lax.all_to_all(soft_query, "head", split_axis=0, concat_axis=1, tiled=True),
        lax.all_to_all(soft_key, "head", split_axis=0, concat_axis=1, tiled=True),
        lax.all_to_all(soft_value, "head", split_axis=0, concat_axis=1, tiled=True),
    )
    query_mine, key_mine, value_mine = (
        lax.all_to_all(query_moved, "ctx", split_axis=1, concat_axis=0, tiled=True),
        lax.all_to_all(key_moved, "ctx", split_axis=1, concat_axis=0, tiled=True),
        lax.all_to_all(value_moved, "ctx", split_axis=1, concat_axis=0, tiled=True),
    )
    query_blocks, query_places, initial = prepare_queries(query_mine, tokens, quarter, head_slot)
    resident_rows = key_mine.shape[0]
    pieces = (
        lax.all_gather(key_mine, "head", axis=0, tiled=True),
        lax.all_gather(value_mine, "head", axis=0, tiled=True),
    )
    key_total = pieces[0].shape[0]
    index_all = jnp.arange(key_total, dtype=jnp.int32)
    source = index_all // resident_rows
    within = index_all % resident_rows
    token_slots = within // quarter * tokens + source * quarter + within % quarter
    result = attend_keys(initial, query_blocks, query_places, pieces[0], pieces[1], token_slots)
    best_final, mass_final, accum_final = result
    outcome = (
        (accum_final / mass_final[..., None]).reshape(query_mine.shape[0], -1).astype(jnp.bfloat16)
    )
    return lax.all_to_all(
        lax.all_to_all(outcome, "ctx", split_axis=0, concat_axis=1, tiled=True),
        "head",
        split_axis=1,
        concat_axis=0,
        tiled=True,
    )


def plain_shards(lin_query, lin_key, lin_value, log_decay, soft_query, soft_key, soft_value):
    lin_out = lightning_core(lin_query, lin_key, lin_value, log_decay)
    soft_out = softmax_core(soft_query, soft_key, soft_value)
    return (lin_out, soft_out)


def shards(lin_query, lin_key, lin_value, log_decay, soft_query, soft_key, soft_value):
    n = lax.axis_size("ctx")
    tokens, columns = lin_query.shape
    heads = log_decay.shape[1]
    half = n // 2
    hp = heads // half
    width = hp * HEAD_DIM
    level_rows = -(-hp // 8) * 8
    vmem = pl.BlockSpec(memory_space=pltpu.VMEM)
    far = pl.BlockSpec(memory_space=pltpu.HBM)
    big = pltpu.VMEM((half * tokens, width), BF16)
    full = pltpu.VMEM((tokens, columns), BF16)
    level = pltpu.VMEM((half, level_rows, tokens), F32)
    some_states = pltpu.VMEM((heads // 2, HEAD_DIM, HEAD_DIM), BF16)
    dma = pltpu.SemaphoreType.DMA
    ring = [dma((half,)), dma((half,))]
    square = [dma((hp, half)), dma((hp, half))]
    single = [dma, dma]
    both = pl.pallas_call(
        functools.partial(kernel, n),
        out_shape=jax.ShapeDtypeStruct((2, tokens, columns), BF16),
        in_specs=[far] * 3 + [vmem] + [far] * 3,
        out_specs=vmem,
        scratch_shapes=[full] * 3 + [big] * 6 + [full] * 2 + [level] * 4
        + [
            pltpu.VMEM((heads, HEAD_DIM, HEAD_DIM), BF16),
            some_states,
            pltpu.VMEM((heads, tokens), F32),
            pltpu.VMEM((heads, tokens), F32),
            some_states,
            pltpu.VMEM((heads, HEAD_DIM, HEAD_DIM), BF16),
            some_states,
            some_states,
            pltpu.VMEM((heads, tokens), F32),
            pltpu.VMEM((tokens, columns), F32),
            dma((6,)),
        ]
        + square * 4 + single * 4 + square + ring + square + ring,
        compiler_params=pltpu.CompilerParams(
            collective_id=0, has_side_effects=True, vmem_limit_bytes=60 * 1024 * 1024
        ),
        cost_estimate=pl.CostEstimate(
            flops=3 * 10**9, bytes_accessed=4 * 10**6, transcendentals=3 * 10**6
        ),
    )(lin_query, lin_key, lin_value, log_decay.T, soft_query, soft_key, soft_value)
    return both[0], both[1]


def solution(mesh):
    spec = P("ctx", "head")
    n = mesh.shape["ctx"]

    def body(*args):
        heads = args[3].shape[1]
        if n % 2 or n < 4 or heads % (n // 2):
            return plain_shards(*args)
        return shards(*args)

    return jax.shard_map(
        body, mesh=mesh, in_specs=(spec,) * 7, out_specs=(spec,) * 2, check_vma=False
    )
```
